512 devices in a mesh: segment: 8 (over x, core), row: 64 (over y, z).
Axes of the slice: x: 4, y: 4, z: 16, core: 2. Of those that a mesh axis runs over, the one named last changes fastest.
Arguments:
- layer_input: bfloat16 [8, 240, 65536], P('segment', None, 'row'), may hold values from 0.0099487305 to 4
- weight_blocks: bfloat16 [8, 512, 16, 128, 128], P('segment', 'row'), may hold values from -0.125 to 0.125
- neuron_bias: float32 [8, 65536], P('segment', 'row'), may hold values from -0.5 to 0.5
- block_slots: int32 [8, 512, 16], P('segment', 'row'), may hold values from 0 to 127, as said below
- send_lists: int32 [8, 64, 64, 2], P('segment', 'row'), may hold values from -1 to 511, as said below
Outputs:
- next_state: bfloat16 [8, 240, 65536], P('segment', None, 'row')
The draws below stay inside these ranges and needn't reach their ends.
Inputs may be any that keep to these rules, and one draw needn't show every extreme that they name: `send_lists`: each entry is -1 or a block of the sending device s, from s * 8 to (s + 1) * 8 - 1; the entries of one sender and receiver are distinct. For each layer and receiving device exactly 64 entries are not -1, and some sender fills all 2 of its slots. `block_slots`: every slot named is a non-empty entry of that device's incoming list; the 16 slots of one block are distinct, and every non-empty slot of a device's list is named by some block of that device.
All inputs are finite; a program needn't handle non-finite values.
Results may differ from the reference program's by a relative error of at most 0.001.
Values may be sent and summed in bfloat16 or wider, within the bound.
No kernel may reach another device: no remote copies, remote signals or barrier semaphores. Data moves between devices by JAX's collectives and lax.ppermute only.
A program may use at most 192 MiB of HBM per device.

```python
import math
import jax
import jax.numpy as jnp
from jax import lax

NEURONS = 65536
BLOCK = 128
K = 16
CAP = 2
SAMPLES = 240
LAYERS = 8
NB = 512
BPD = 8
NEED = 64
N_ROW = 64


def build_plan(key):
    base = jax.random.fold_in(key, 11)
    key_hot, key_rank, key_local, key_shuffle = jax.random.split(base, 4)
    span = N_ROW * CAP
    candidate = jnp.arange(span, dtype=jnp.int32)
    hot_source = jax.random.randint(key_hot, (LAYERS, N_ROW, 1), 0, N_ROW)
    scores = jax.random.randint(key_rank, (LAYERS, N_ROW, span), 0, 1 << 20)
    scores = jnp.where((candidate // CAP)[None, None, :] == hot_source, -1, scores)
    ranking = jnp.argsort(scores * span + candidate[None, None, :], axis=-1).astype(jnp.int32)
    chosen = ranking[..., :NEED]
    selected = jnp.any(chosen[..., :, None] == candidate[None, None, None, :], axis=-2)
    local_scores = jax.random.randint(key_local, (LAYERS, N_ROW, N_ROW, BPD), 0, 1 << 20)
    local_scores = local_scores * BPD + jnp.arange(BPD, dtype=jnp.int32)
    local_pick = jnp.argsort(local_scores, axis=-1).astype(jnp.int32)[..., :CAP]
    owner_base = jnp.arange(N_ROW, dtype=jnp.int32)[None, None, :, None] * BPD
    block_ids = local_pick + owner_base
    by_receiver = jnp.where(selected.reshape(LAYERS, N_ROW, N_ROW, CAP), block_ids, -1)
    outgoing = jnp.transpose(by_receiver, (0, 2, 1, 3)).astype(jnp.int32)
    shuffle_scores = jax.random.randint(key_shuffle, (LAYERS, N_ROW, NEED), 0, 1 << 20)
    shuffle_scores = shuffle_scores * NEED + jnp.arange(NEED, dtype=jnp.int32)
    shuffle = jnp.argsort(shuffle_scores, axis=-1).astype(jnp.int32)
    needed = jnp.take_along_axis(chosen, shuffle, axis=-1)
    use_index = (jnp.arange(BPD, dtype=jnp.int32)[:, None] * K + jnp.arange(K, dtype=jnp.int32)[None, :]) % NEED
    slot_table = needed[:, :, use_index]
    return (outgoing, slot_table.reshape(LAYERS, N_ROW * BPD, K).astype(jnp.int32))


def draw_block_slots(key, part):
    return build_plan(key)[1]


def draw_send_lists(key, part):
    return build_plan(key)[0]


def steps_of(own_key, shape, cuts, least, top_value):
    def one(dim, parts):
        steps = jax.random.uniform(jax.random.fold_in(jax.random.fold_in(own_key, 6), dim), (parts,), jnp.float32, least / len(cuts), top_value / len(cuts))
        return jnp.repeat(jnp.exp(steps), shape[dim] // parts).reshape((-1,) + (1,) * (len(shape) - dim - 1))

    gain = one(*cuts[0])
    for cut in cuts[1:]:
        gain = gain * one(*cut)
    return gain


def bell_draw(rng, dims, deviation, bound, cuts=(), kind=jnp.bfloat16):
    drawn = jax.random.normal(rng, dims, jnp.float32) * deviation
    if len(cuts) > 0:
        drawn = steps_of(rng, dims, cuts, -0.22, 0.18) * drawn
    return jnp.clip(drawn, min=-bound, max=bound).astype(kind)


def setup_inputs(seed: int = 0) -> dict:
    keys = jax.random.split(jax.random.key(seed), 6)
    return {
        "layer_input": jnp.clip(jnp.exp(math.log(4.0) - 5.996605 * jax.random.uniform(keys[0], (LAYERS, SAMPLES, NEURONS), jnp.float32) ** steps_of(keys[0], (LAYERS, SAMPLES, NEURONS), ((0, 8), (2, 64)), -0.2, 0.2)), 0.0099487305, 4.0).astype(jnp.bfloat16),
        "weight_blocks": bell_draw(keys[1], (LAYERS, NB, K, BLOCK, BLOCK), (K * BLOCK) ** -0.5, 0.125, ((0, 8), (1, 64))),
        "neuron_bias": jnp.clip(jax.random.uniform(keys[2], (LAYERS, NEURONS), jnp.float32, -0.5, 0.5) * steps_of(keys[2], (LAYERS, NEURONS), ((0, 8), (1, 64)), -0.4, 0.0), -0.5, 0.5),
        "block_slots": draw_block_slots(jax.random.fold_in(keys[5], 71), 0),
        "send_lists": draw_send_lists(jax.random.fold_in(keys[5], 71), 0),
    }


CLAMP_TOP = 3.0


def section(layer_input, weight_blocks, neuron_bias, block_slots, send_lists):
    sample_count = layer_input.shape[0]
    incoming = jnp.transpose(send_lists, (1, 0, 2)).reshape(N_ROW, N_ROW * CAP)
    owner_row = jnp.arange(NB, dtype=jnp.int32) // BPD
    rows_in = jnp.take(incoming, owner_row, axis=0)
    source = jnp.take_along_axis(rows_in, block_slots, axis=1).astype(jnp.int32)
    blocks = layer_input.reshape(sample_count, NB, BLOCK)
    picked = jnp.take(blocks, source.reshape(-1), axis=1).reshape(sample_count, NB, K, BLOCK)
    mixed = jnp.einsum("mjkb,jkbc->mjc", picked.astype(jnp.float32), weight_blocks.astype(jnp.float32))
    result = mixed.reshape(sample_count, NEURONS) + neuron_bias
    return jnp.clip(result, 0.0, CLAMP_TOP).astype(jnp.bfloat16)


def reference(layer_input, weight_blocks, neuron_bias, block_slots, send_lists):
    layer_out = lax.map(lambda packed: section(*packed), (layer_input, weight_blocks, neuron_bias, block_slots, send_lists))
    return jnp.roll(layer_out, 1, axis=0)
```

```python
import jax
import jax.numpy as jnp
from jax import lax
from jax.experimental import pallas as pl
from jax.experimental.pallas import tpu as pltpu
from jax.sharding import Mesh, PartitionSpec as P

CLAMP_TOP = 3.0
LINES = 4
STEPS = 16
CAP = 2
BLOCK = 128


def pick_kernel(ids_ref, line_ref, out_ref, sem):
    slots = STEPS * CAP

    def start(i, carry):
        z = i // (LINES * CAP)
        y = (i // CAP) % LINES
        c = i % CAP
        block = ids_ref[i] & 7
        columns = pl.ds(pl.multiple_of(block * BLOCK, BLOCK), BLOCK)
        pltpu.make_async_copy(
            line_ref.at[z, :, columns], out_ref.at[y * slots + z * CAP + c], sem
        ).start()
        return carry

    lax.fori_loop(0, STEPS * LINES * CAP, start, 0)
    pltpu.make_async_copy(out_ref, out_ref, sem).wait()


def pick(ids, line):
    rows = line.shape[1]
    count = LINES * STEPS * CAP
    return pl.pallas_call(
        pick_kernel,
        grid_spec=pltpu.PrefetchScalarGridSpec(
            num_scalar_prefetch=1,
            grid=(1,),
            in_specs=[pl.BlockSpec(memory_space=pl.ANY)],
            out_specs=pl.BlockSpec(memory_space=pl.ANY),
            scratch_shapes=[pltpu.SemaphoreType.DMA],
        ),
        out_shape=jax.ShapeDtypeStruct((count, rows, BLOCK), jnp.bfloat16),
        cost_estimate=pl.CostEstimate(
            flops=0, bytes_accessed=2 * count * rows * BLOCK * 2, transcendentals=0
        ),
        name="pick",
    )(ids, line)


def mix_kernel(slots_ref, blocks_ref, weight_ref, bias_ref, out_ref, held, sems):
    j = pl.program_id(0)
    per_device = pl.num_programs(0)
    taps = weight_ref.shape[1]

    def fetch(which, into):
        for k in range(taps):
            pltpu.make_async_copy(
                blocks_ref.at[slots_ref[which * taps + k]],
                held.at[into, :, k * BLOCK : (k + 1) * BLOCK],
                sems.at[into],
            ).start()

    @pl.when(j == 0)
    def _():
        fetch(0, 0)

    @pl.when(j + 1 < per_device)
    def _():
        fetch(j + 1, (j + 1) % 2)

    now = j % 2
    pltpu.make_async_copy(held.at[now], held.at[now], sems.at[now]).wait()
    weights = weight_ref[0].reshape(taps * BLOCK, BLOCK)
    mixed = jnp.dot(held[now], weights, preferred_element_type=jnp.float32)
    result = mixed + bias_ref[0]
    out_ref[...] = jnp.clip(result, 0.0, CLAMP_TOP).astype(jnp.bfloat16)


def mix(slots, blocks, weights, bias):
    per_device, taps = weights.shape[:2]
    rows = blocks.shape[1]
    return pl.pallas_call(
        mix_kernel,
        grid_spec=pltpu.PrefetchScalarGridSpec(
            num_scalar_prefetch=1,
            grid=(per_device,),
            in_specs=[
                pl.BlockSpec(memory_space=pl.ANY),
                pl.BlockSpec((1, taps, BLOCK, BLOCK), lambda j, s: (j, 0, 0, 0)),
                pl.BlockSpec((1, 1, BLOCK), lambda j, s: (j, 0, 0)),
            ],
            out_specs=pl.BlockSpec((rows, BLOCK), lambda j, s: (0, j)),
            scratch_shapes=[
                pltpu.VMEM((2, rows, taps * BLOCK), jnp.bfloat16),
                pltpu.SemaphoreType.DMA((2,)),
            ],
        ),
        out_shape=jax.ShapeDtypeStruct((rows, per_device * BLOCK), jnp.bfloat16),
        compiler_params=pltpu.CompilerParams(vmem_limit_bytes=16 * 2**20),
        cost_estimate=pl.CostEstimate(
            flops=2 * rows * per_device * taps * BLOCK * BLOCK,
            bytes_accessed=per_device * taps * (rows + BLOCK) * BLOCK * 2,
            transcendentals=0,
        ),
        name="mix",
    )(slots, blocks, weights, bias.reshape(per_device, 1, BLOCK))


def body(layer_input, weight_blocks, neuron_bias, block_slots, send_lists):
    samples = layer_input[0]
    lists = send_lists.reshape(LINES, STEPS, CAP).transpose(1, 0, 2)
    ids = lax.all_to_all(lists, "z", 0, 0, tiled=True).reshape(-1)
    line = lax.all_gather(samples, "z")
    outgoing = pick(ids, line)
    incoming = lax.all_to_all(outgoing, "y", 0, 0, tiled=True)
    out = mix(block_slots.reshape(-1), incoming, weight_blocks[0], neuron_bias[0])
    count = lax.axis_size("segment")
    shifted = lax.ppermute(out, "segment", [(i, (i + 1) % count) for i in range(count)])
    return shifted[None]


def solution(mesh):
    segments, row = mesh.devices.shape
    split = Mesh(
        mesh.devices.reshape(segments, row // STEPS, STEPS), ("segment", "y", "z")
    )
    row = ("y", "z")
    placed = (
        P("segment", None, row),
        P("segment", row, None, None, None),
        P("segment", row),
        P("segment", row, None),
        P("segment", row, None, None),
    )
    return jax.shard_map(
        body,
        mesh=split,
        in_specs=placed,
        out_specs=P("segment", None, row),
        check_vma=False,
    )
```

```python
import jax
import jax.numpy as jnp
from jax import lax
from jax.experimental import pallas as pl
from jax.experimental.pallas import tpu as pltpu
from jax.sharding import Mesh, PartitionSpec as P

CLAMP_TOP = 3.0
LINES = 4
STEPS = 16
CAP = 2
BLOCK = 128


def pick_kernel(ids_ref, line_ref, out_ref, sem):
    y = pl.program_id(0)

    def start(i, carry):
        z = i // CAP
        block = ids_ref[(z * LINES + y) * CAP + i % CAP] & 7
        columns = pl.ds(pl.multiple_of(block * BLOCK, BLOCK), BLOCK)
        pltpu.make_async_copy(line_ref.at[z, :, columns], out_ref.at[i], sem).start()
        return carry

    lax.fori_loop(0, STEPS * CAP, start, 0)
    pltpu.make_async_copy(out_ref, out_ref, sem).wait()


def pick(ids, line):
    rows = line.shape[1]
    count = STEPS * CAP
    return pl.pallas_call(
        pick_kernel,
        grid_spec=pltpu.PrefetchScalarGridSpec(
            num_scalar_prefetch=1,
            grid=(LINES,),
            in_specs=[pl.BlockSpec(memory_space=pl.ANY)],
            out_specs=pl.BlockSpec((count, rows, BLOCK), lambda y, ids: (y, 0, 0)),
            scratch_shapes=[pltpu.SemaphoreType.DMA],
        ),
        out_shape=jax.ShapeDtypeStruct((LINES * count, rows, BLOCK), jnp.bfloat16),
        compiler_params=pltpu.CompilerParams(vmem_limit_bytes=16 * 2**20),
        cost_estimate=pl.CostEstimate(
            flops=0,
            bytes_accessed=2 * LINES * count * rows * BLOCK * 2,
            transcendentals=0,
        ),
        name="pick",
    )(ids, line)


def mix_kernel(slots_ref, blocks_ref, weight_ref, bias_ref, out_ref, held, sems):
    j = pl.program_id(0)
    per_device = pl.num_programs(0)
    taps = weight_ref.shape[1]

    def fetch(which, into):
        for k in range(taps):
            pltpu.make_async_copy(
                blocks_ref.at[slots_ref[which * taps + k]],
                held.at[into, :, k * BLOCK : (k + 1) * BLOCK],
                sems.at[into],
            ).start()

    @pl.when(j == 0)
    def _():
        fetch(0, 0)

    @pl.when(j + 1 < per_device)
    def _():
        fetch(j + 1, (j + 1) % 2)

    now = j % 2
    pltpu.make_async_copy(held.at[now], held.at[now], sems.at[now]).wait()
    weights = weight_ref[0].reshape(taps * BLOCK, BLOCK)
    mixed = jnp.dot(held[now], weights, preferred_element_type=jnp.float32)
    result = mixed + bias_ref[0]
    out_ref[...] = jnp.clip(result, 0.0, CLAMP_TOP).astype(jnp.bfloat16)


def mix(slots, blocks, weights, bias):
    per_device, taps = weights.shape[:2]
    rows = blocks.shape[1]
    return pl.pallas_call(
        mix_kernel,
        grid_spec=pltpu.PrefetchScalarGridSpec(
            num_scalar_prefetch=1,
            grid=(per_device,),
            in_specs=[
                pl.BlockSpec(memory_space=pl.ANY),
                pl.BlockSpec((1, taps, BLOCK, BLOCK), lambda j, s: (j, 0, 0, 0)),
                pl.BlockSpec((1, 1, BLOCK), lambda j, s: (j, 0, 0)),
            ],
            out_specs=pl.BlockSpec((rows, BLOCK), lambda j, s: (0, j)),
            scratch_shapes=[
                pltpu.VMEM((2, rows, taps * BLOCK), jnp.bfloat16),
                pltpu.SemaphoreType.DMA((2,)),
            ],
        ),
        out_shape=jax.ShapeDtypeStruct((rows, per_device * BLOCK), jnp.bfloat16),
        compiler_params=pltpu.CompilerParams(vmem_limit_bytes=16 * 2**20),
        cost_estimate=pl.CostEstimate(
            flops=2 * rows * per_device * taps * BLOCK * BLOCK,
            bytes_accessed=per_device * taps * (rows + BLOCK) * BLOCK * 2,
            transcendentals=0,
        ),
        name="mix",
    )(slots, blocks, weights, bias.reshape(per_device, 1, BLOCK))


def body(layer_input, weight_blocks, neuron_bias, block_slots, send_lists):
    samples = layer_input[0]
    lists = send_lists.reshape(LINES, STEPS, CAP).transpose(1, 0, 2)
    ids = lax.all_to_all(lists, "z", 0, 0, tiled=True).reshape(-1)
    line = lax.all_gather(samples, "z")
    outgoing = pick(ids, line)
    incoming = lax.all_to_all(outgoing, "y", 0, 0, tiled=True)
    out = mix(block_slots.reshape(-1), incoming, weight_blocks[0], neuron_bias[0])
    count = lax.axis_size("segment")
    shifted = lax.ppermute(out, "segment", [(i, (i + 1) % count) for i in range(count)])
    return shifted[None]


def solution(mesh):
    segments, row = mesh.devices.shape
    split = Mesh(
        mesh.devices.reshape(segments, row // STEPS, STEPS), ("segment", "y", "z")
    )
    row = ("y", "z")
    placed = (
        P("segment", None, row),
        P("segment", row, None, None, None),
        P("segment", row),
        P("segment", row, None),
        P("segment", row, None, None),
    )
    return jax.shard_map(
        body,
        mesh=split,
        in_specs=placed,
        out_specs=P("segment", None, row),
        check_vma=False,
    )
```

```python
import jax
import jax.numpy as jnp
from jax import lax
from jax.experimental import pallas as pl
from jax.experimental.pallas import tpu as pltpu
from jax.sharding import Mesh, PartitionSpec as P

CLAMP_TOP = 3.0
LINES = 4
STEPS = 16
CAP = 2
BLOCK = 128
KERNEL_VMEM = 24 * 2**20
RING = 160
LATE = 7
PARTS = (
    (0, -1, 1, -2, 2),
    (-3, 3, -4, 4),
    (-5, 5, -6, 6),
    (-7, 7, 8),
)


def copy_blocks(ids_ref, senders, out_ref, held, in_sems, out_sem):
    for y in range(LINES):
        for i, (z, pieces) in enumerate(senders):
            for c in range(CAP):
                block = ids_ref[(z * LINES + y) * CAP + c] & 7
                columns = pl.ds(pl.multiple_of(block * BLOCK, BLOCK), BLOCK)
                for ref, first in pieces:
                    rows = pl.ds(first, ref.shape[0])
                    pltpu.make_async_copy(
                        ref.at[:, columns], held.at[y, i * CAP + c, rows], in_sems.at[y]
                    ).start()
    for y in range(LINES):
        pltpu.make_async_copy(held.at[y], held.at[y], in_sems.at[y]).wait()
        pltpu.make_async_copy(held.at[y], out_ref.at[y], out_sem).start()
    pltpu.make_async_copy(held, held, out_sem).wait()


def pick_call(kernel, scalars, operands, count, rows, name):
    shape = (LINES, count, rows, BLOCK)
    size = LINES * count * rows * BLOCK * 2
    return pl.pallas_call(
        kernel,
        grid_spec=pltpu.PrefetchScalarGridSpec(
            num_scalar_prefetch=len(scalars),
            grid=(1,),
            in_specs=[pl.BlockSpec(memory_space=pltpu.HBM)] * len(operands),
            out_specs=pl.BlockSpec(memory_space=pltpu.HBM),
            scratch_shapes=[
                pltpu.VMEM(shape, jnp.bfloat16),
                pltpu.SemaphoreType.DMA((LINES,)),
                pltpu.SemaphoreType.DMA,
            ],
        ),
        out_shape=jax.ShapeDtypeStruct(shape, jnp.bfloat16),
        compiler_params=pltpu.CompilerParams(vmem_limit_bytes=KERNEL_VMEM),
        cost_estimate=pl.CostEstimate(
            flops=0, bytes_accessed=2 * size, transcendentals=0
        ),
        name=name,
    )(*scalars, *operands)


def pick_part(ids, here, part, pieces, rows):
    flat = [array for ps in pieces for array, _ in ps]

    def kernel(ids_ref, here_ref, *refs):
        sources, (out_ref, held, in_sems, out_sem) = refs[:-4], refs[-4:]
        senders, at = [], 0
        for offset, ps in zip(part, pieces):
            z = (here_ref[0] + (offset + STEPS)) & (STEPS - 1)
            senders.append((z, [(sources[at + n], f) for n, (_, f) in enumerate(ps)]))
            at += len(ps)
        copy_blocks(ids_ref, senders, out_ref, held, in_sems, out_sem)

    return pick_call(kernel, (ids, here), flat, len(part) * CAP, rows, "pick_part")


def pick_line(ids, line):
    def kernel(ids_ref, line_ref, out_ref, held, in_sems, out_sem):
        senders = [(z, [(line_ref.at[z], 0)]) for z in range(STEPS)]
        copy_blocks(ids_ref, senders, out_ref, held, in_sems, out_sem)

    return pick_call(kernel, (ids,), (line,), STEPS * CAP, line.shape[1], "pick_line")


def mix(codes, arrays, weights, bias):
    per_device, taps = weights.shape[:2]
    rows = arrays[0].shape[1]

    def kernel(codes_ref, *refs):
        blocks_refs = refs[: len(arrays)]
        weight_ref, bias_ref, out_ref, held, sems = refs[len(arrays) :]
        j = pl.program_id(0)

        def fetch(which, into):
            for k in range(taps):
                code = codes_ref[which * taps + k]
                for a, ref in enumerate(blocks_refs):

                    def go(ref=ref, k=k, code=code):
                        pltpu.make_async_copy(
                            ref.at[code & 255],
                            held.at[into, :, k * BLOCK : (k + 1) * BLOCK],
                            sems.at[into],
                        ).start()

                    if len(blocks_refs) == 1:
                        go()
                    else:
                        pl.when((code >> 8) == a)(go)

        @pl.when(j == 0)
        def _():
            fetch(0, 0)

        @pl.when(j + 1 < per_device)
        def _():
            fetch(j + 1, (j + 1) % 2)

        now = j % 2
        pltpu.make_async_copy(held.at[now], held.at[now], sems.at[now]).wait()
        stacked = weight_ref[0].reshape(taps * BLOCK, BLOCK)
        mixed = jnp.dot(held[now], stacked, preferred_element_type=jnp.float32)
        result = mixed + bias_ref[0]
        out_ref[...] = jnp.clip(result, 0.0, CLAMP_TOP).astype(jnp.bfloat16)

    return pl.pallas_call(
        kernel,
        grid_spec=pltpu.PrefetchScalarGridSpec(
            num_scalar_prefetch=1,
            grid=(per_device,),
            in_specs=[pl.BlockSpec(memory_space=pltpu.HBM)] * len(arrays)
            + [
                pl.BlockSpec((1, taps, BLOCK, BLOCK), lambda j, s: (j, 0, 0, 0)),
                pl.BlockSpec((1, 1, BLOCK), lambda j, s: (j, 0, 0)),
            ],
            out_specs=pl.BlockSpec((rows, BLOCK), lambda j, s: (0, j)),
            scratch_shapes=[
                pltpu.VMEM((2, rows, taps * BLOCK), jnp.bfloat16),
                pltpu.SemaphoreType.DMA((2,)),
            ],
        ),
        out_shape=jax.ShapeDtypeStruct((rows, per_device * BLOCK), jnp.bfloat16),
        compiler_params=pltpu.CompilerParams(vmem_limit_bytes=KERNEL_VMEM),
        cost_estimate=pl.CostEstimate(
            flops=2 * rows * per_device * taps * BLOCK * BLOCK,
            bytes_accessed=per_device * taps * (rows + BLOCK) * BLOCK * 2,
            transcendentals=0,
        ),
        name="mix",
    )(codes, *arrays, weights, bias.reshape(per_device, 1, BLOCK))


def shifted(value, axis, by):
    count = lax.axis_size(axis)
    return lax.ppermute(value, axis, [(i, (i + by) % count) for i in range(count)])


def over_lines(outgoing):
    incoming = lax.all_to_all(outgoing, "y", 0, 0, tiled=True)
    return incoming.reshape((-1,) + incoming.shape[2:])


def part_codes(slots, here):
    line, z, c = slots >> 5, (slots >> 1) & (STEPS - 1), slots & 1
    offset = (z - here) & (STEPS - 1)
    codes = jnp.zeros_like(slots)
    for p, part in enumerate(PARTS):
        for i, o in enumerate(part):
            code = p * 256 + line * (len(part) * CAP) + i * CAP + c
            codes = jnp.where(offset == o % STEPS, code, codes)
    return codes


def body(layer_input, weight_blocks, neuron_bias, block_slots, send_lists):
    samples, weights, bias = layer_input[0], weight_blocks[0], neuron_bias[0]
    slots = block_slots.reshape(-1)
    here = lax.axis_index("z").astype(jnp.int32)
    rest = samples[RING:]
    ring = samples[:RING]

    line = lax.all_gather(rest, "z")
    lists = send_lists.reshape(LINES, STEPS, CAP).transpose(1, 0, 2)
    ids = lax.all_to_all(lists, "z", 0, 0, tiled=True).reshape(-1)

    held = {0: [(ring, 0)]}
    up = down = ring
    for step in range(1, STEPS // 2):
        if step == 2:
            ids, up, down = lax.optimization_barrier((ids, up, down))
        if step == LATE:
            line, up, down = lax.optimization_barrier((line, up, down))
        up, down = shifted(up, "z", 1), shifted(down, "z", -1)
        held[-step], held[step] = [(up, 0)], [(down, 0)]
    half = RING // 2
    held[STEPS // 2] = [
        (shifted(up[:half], "z", 1), 0),
        (shifted(down[half:], "z", -1), half),
    ]

    arrived = []
    for part in PARTS:
        pieces = [held[o] for o in part]
        picked = pick_part(ids, here.reshape(1), part, pieces, RING)
        arrived.append(over_lines(picked))
    arrived_rest = over_lines(pick_line(ids, line))

    out_rest = shifted(mix(slots, [arrived_rest], weights, bias), "segment", 1)
    codes = part_codes(slots, here)
    out_ring = shifted(mix(codes, arrived, weights, bias), "segment", 1)
    return jnp.concatenate([out_ring, out_rest], axis=0)[None]


def solution(mesh):
    segments, row = mesh.devices.shape
    split = Mesh(
        mesh.devices.reshape(segments, row // STEPS, STEPS), ("segment", "y", "z")
    )
    row = ("y", "z")
    placed = (
        P("segment", None, row),
        P("segment", row, None, None, None),
        P("segment", row),
        P("segment", row, None),
        P("segment", row, None, None),
    )
    return jax.shard_map(
        body,
        mesh=split,
        in_specs=placed,
        out_specs=P("segment", None, row),
        check_vma=False,
    )
```

```python
import jax
import jax.numpy as jnp
from jax import lax
from jax.experimental import pallas as pl
from jax.experimental.pallas import tpu as pltpu
from jax.sharding import Mesh, PartitionSpec as P

CLAMP_TOP = 3.0
LINES = 4
STEPS = 16
CAP = 2
BLOCK = 128
PICK_VMEM = 24 * 2**20
MIX_VMEM = 58 * 2**20
PICK_WEIGHT = 12 * 10**9
IDS_STEP = 2
MIX_WEIGHT = 40
TIE = 4
LATE = 7
RING = 160
PARTS = (
    (0, -1, 1),
    (-2, 2, -3, 3),
    (-4, 4, -5, 5),
    (-6, 6, -7, 7, 8),
)


def copy_blocks(ids_ref, senders, out_ref, held, in_sems, out_sem):
    for y in range(LINES):
        for i, (z, pieces) in enumerate(senders):
            for c in range(CAP):
                block = ids_ref[(z * LINES + y) * CAP + c] & 7
                columns = pl.ds(pl.multiple_of(block * BLOCK, BLOCK), BLOCK)
                for ref, first in pieces:
                    rows = pl.ds(first, ref.shape[0])
                    pltpu.make_async_copy(
                        ref.at[:, columns], held.at[y, i * CAP + c, rows], in_sems.at[y]
                    ).start()
    for y in range(LINES):
        pltpu.make_async_copy(held.at[y], held.at[y], in_sems.at[y]).wait()
        pltpu.make_async_copy(held.at[y], out_ref.at[y], out_sem).start()
    pltpu.make_async_copy(held, held, out_sem).wait()


def pick_call(kernel, scalars, operands, count, rows, name):
    shape = (LINES, count, rows, BLOCK)
    size = LINES * count * rows * BLOCK * 2
    return pl.pallas_call(
        kernel,
        grid_spec=pltpu.PrefetchScalarGridSpec(
            num_scalar_prefetch=len(scalars),
            grid=(1,),
            in_specs=[pl.BlockSpec(memory_space=pltpu.HBM)] * len(operands),
            out_specs=pl.BlockSpec(memory_space=pltpu.HBM),
            scratch_shapes=[
                pltpu.VMEM(shape, jnp.bfloat16),
                pltpu.SemaphoreType.DMA((LINES,)),
                pltpu.SemaphoreType.DMA,
            ],
        ),
        out_shape=jax.ShapeDtypeStruct(shape, jnp.bfloat16),
        compiler_params=pltpu.CompilerParams(vmem_limit_bytes=PICK_VMEM),
        cost_estimate=pl.CostEstimate(
            flops=PICK_WEIGHT, bytes_accessed=2 * size, transcendentals=0
        ),
        name=name,
    )(*scalars, *operands)


def pick_part(ids, here, part, pieces, rows):
    flat = [array for ps in pieces for array, _ in ps]

    def kernel(ids_ref, here_ref, *refs):
        sources, (out_ref, held, in_sems, out_sem) = refs[:-4], refs[-4:]
        senders, at = [], 0
        for offset, ps in zip(part, pieces):
            z = (here_ref[0] + (offset + STEPS)) & (STEPS - 1)
            senders.append((z, [(sources[at + n], f) for n, (_, f) in enumerate(ps)]))
            at += len(ps)
        copy_blocks(ids_ref, senders, out_ref, held, in_sems, out_sem)

    return pick_call(kernel, (ids, here), flat, len(part) * CAP, rows, "pick_part")


def pick_line(ids, line):
    def kernel(ids_ref, line_ref, out_ref, held, in_sems, out_sem):
        senders = [(z, [(line_ref.at[z], 0)]) for z in range(STEPS)]
        copy_blocks(ids_ref, senders, out_ref, held, in_sems, out_sem)

    return pick_call(kernel, (ids,), (line,), STEPS * CAP, line.shape[1], "pick_line")


def mix(codes, arrays, weights, bias, weight=1):
    per_device, taps = weights.shape[:2]
    rows = arrays[0].shape[1]

    def kernel(codes_ref, *refs):
        blocks_refs = refs[: len(arrays)]
        weight_ref, bias_ref, out_ref, held, sems = refs[len(arrays) :]
        j = pl.program_id(0)

        def fetch(which, into):
            def choose(code, k, first, last):
                if last - first == 1:
                    pltpu.make_async_copy(
                        blocks_refs[first].at[code & 255],
                        held.at[into, :, k * BLOCK : (k + 1) * BLOCK],
                        sems.at[into],
                    ).start()
                    return
                middle = (first + last) // 2
                low = (code >> 8) < middle
                pl.when(low)(lambda: choose(code, k, first, middle))
                pl.when(jnp.logical_not(low))(lambda: choose(code, k, middle, last))

            for k in range(taps):
                choose(codes_ref[which * taps + k], k, 0, len(blocks_refs))

        @pl.when(j == 0)
        def _():
            fetch(0, 0)

        @pl.when(j + 1 < per_device)
        def _():
            fetch(j + 1, (j + 1) % 2)

        now = j % 2
        pltpu.make_async_copy(held.at[now], held.at[now], sems.at[now]).wait()
        stacked = weight_ref[0].reshape(taps * BLOCK, BLOCK)
        mixed = jnp.dot(held[now], stacked, preferred_element_type=jnp.float32)
        result = mixed + bias_ref[0]
        out_ref[...] = jnp.clip(result, 0.0, CLAMP_TOP).astype(jnp.bfloat16)

    return pl.pallas_call(
        kernel,
        grid_spec=pltpu.PrefetchScalarGridSpec(
            num_scalar_prefetch=1,
            grid=(per_device,),
            in_specs=[pl.BlockSpec(memory_space=pltpu.HBM)] * len(arrays)
            + [
                pl.BlockSpec((1, taps, BLOCK, BLOCK), lambda j, s: (j, 0, 0, 0)),
                pl.BlockSpec((1, 1, BLOCK), lambda j, s: (j, 0, 0)),
            ],
            out_specs=pl.BlockSpec((rows, BLOCK), lambda j, s: (0, j)),
            scratch_shapes=[
                pltpu.VMEM((2, rows, taps * BLOCK), jnp.bfloat16),
                pltpu.SemaphoreType.DMA((2,)),
            ],
        ),
        out_shape=jax.ShapeDtypeStruct((rows, per_device * BLOCK), jnp.bfloat16),
        compiler_params=pltpu.CompilerParams(vmem_limit_bytes=MIX_VMEM),
        cost_estimate=pl.CostEstimate(
            flops=weight * 2 * rows * per_device * taps * BLOCK * BLOCK,
            bytes_accessed=per_device * taps * (rows + BLOCK) * BLOCK * 2,
            transcendentals=0,
        ),
        name="mix",
    )(codes, *arrays, weights, bias.reshape(per_device, 1, BLOCK))


def shifted(value, axis, by):
    count = lax.axis_size(axis)
    return lax.ppermute(value, axis, [(i, (i + by) % count) for i in range(count)])


def over_lines(outgoing):
    incoming = lax.all_to_all(outgoing, "y", 0, 0, tiled=True)
    return incoming.reshape((-1,) + incoming.shape[2:])


def part_codes(slots, here):
    line, z, c = slots >> 5, (slots >> 1) & (STEPS - 1), slots & 1
    offset = (z - here) & (STEPS - 1)
    codes = jnp.zeros_like(slots)
    for p, part in enumerate(PARTS):
        for i, o in enumerate(part):
            code = p * 256 + line * (len(part) * CAP) + i * CAP + c
            codes = jnp.where(offset == o % STEPS, code, codes)
    return codes


def body(layer_input, weight_blocks, neuron_bias, block_slots, send_lists):
    samples, weights, bias = layer_input[0], weight_blocks[0], neuron_bias[0]
    slots = block_slots.reshape(-1)
    here = lax.axis_index("z").astype(jnp.int32)
    rest = samples[RING:]
    ring = samples[:RING]

    line = lax.all_gather(rest, "z")
    lists = send_lists.reshape(LINES, STEPS, CAP).transpose(1, 0, 2)

    held = {0: [(ring, 0)]}
    up = down = ring
    picked, arrived = [], []

    def pick_next():
        part = PARTS[len(picked)]
        pieces = [held[o] for o in part]
        picked.append(pick_part(ids, here.reshape(1), part, pieces, RING))

    def send_next():
        arrived.append(over_lines(picked[len(arrived)]))

    ids = lax.all_to_all(lists, "z", 0, 0, tiled=True).reshape(-1)
    last = STEPS // 2
    half = RING // 32 * 16
    waiting = []
    for step in range(1, last + 1):
        if step == IDS_STEP:
            ids, up, down = lax.optimization_barrier((ids, up, down))
        if step == LATE:
            line, up, down = lax.optimization_barrier((line, up, down))
            picked_rest = pick_line(ids, line)
            arrived_rest = over_lines(picked_rest)
        for ready, index in waiting:
            if step == ready + 2:
                picked[index], up, down = lax.optimization_barrier(
                    (picked[index], up, down)
                )
                send_next()
            if step == ready + TIE:
                arrived[index], up, down = lax.optimization_barrier(
                    (arrived[index], up, down)
                )
        if step < last:
            up, down = shifted(up, "z", 1), shifted(down, "z", -1)
            held[-step], held[step] = [(up, 0)], [(down, 0)]
        else:
            up, down = shifted(up[:half], "z", 1), shifted(down[half:], "z", -1)
            arrived_rest, up, down = lax.optimization_barrier((arrived_rest, up, down))
            held[step] = [(up, 0), (down, half)]
        if all(o in held for o in PARTS[len(picked)]):
            waiting.append((step, len(picked)))
            pick_next()
    send_next()

    out_rest = shifted(mix(slots, [arrived_rest], weights, bias, MIX_WEIGHT), "segment", 1)
    codes = part_codes(slots, here)
    out_ring = shifted(mix(codes, arrived, weights, bias), "segment", 1)
    return jnp.concatenate([out_ring, out_rest], axis=0)[None]


def solution(mesh):
    segments, row = mesh.devices.shape
    split = Mesh(
        mesh.devices.reshape(segments, row // STEPS, STEPS), ("segment", "y", "z")
    )
    row = ("y", "z")
    placed = (
        P("segment", None, row),
        P("segment", row, None, None, None),
        P("segment", row),
        P("segment", row, None),
        P("segment", row, None, None),
    )
    return jax.shard_map(
        body,
        mesh=split,
        in_specs=placed,
        out_specs=P("segment", None, row),
        check_vma=False,
    )
```

```python
import jax
import jax.numpy as jnp
from jax import lax
from jax.experimental import pallas as pl
from jax.experimental.pallas import tpu as pltpu
from jax.sharding import Mesh, PartitionSpec as P

CLAMP_TOP = 3.0
LINES = 4
STEPS = 16
CAP = 2
BLOCK = 128
PICK_VMEM = 24 * 2**20
MIX_VMEM = 58 * 2**20
PICK_WEIGHT = 12 * 10**9
IDS_STEP = 2
HAVE = (5,7,8, 9, 9)
PARTS = (
    (0, -1, 1),
    (-2, 2, -3, 3),
    (-4, 4, -5, 5),
    (-6, 6),
    (-7, 7, 8),
)


def copy_blocks(ids_ref, senders, out_ref, held, in_sems, out_sem):
    for y in range(LINES):
        for i, (z, pieces) in enumerate(senders):
            for c in range(CAP):
                block = ids_ref[(z * LINES + y) * CAP + c] & 7
                columns = pl.ds(pl.multiple_of(block * BLOCK, BLOCK), BLOCK)
                for ref, first in pieces:
                    rows = pl.ds(first, ref.shape[0])
                    pltpu.make_async_copy(
                        ref.at[:, columns], held.at[y, i * CAP + c, rows], in_sems.at[y]
                    ).start()
    for y in range(LINES):
        pltpu.make_async_copy(held.at[y], held.at[y], in_sems.at[y]).wait()
        pltpu.make_async_copy(held.at[y], out_ref.at[y], out_sem).start()
    pltpu.make_async_copy(held, held, out_sem).wait()


def pick_call(kernel, scalars, operands, count, rows, name):
    shape = (LINES, count, rows, BLOCK)
    size = LINES * count * rows * BLOCK * 2
    return pl.pallas_call(
        kernel,
        grid_spec=pltpu.PrefetchScalarGridSpec(
            num_scalar_prefetch=len(scalars),
            grid=(1,),
            in_specs=[pl.BlockSpec(memory_space=pltpu.HBM)] * len(operands),
            out_specs=pl.BlockSpec(memory_space=pltpu.HBM),
            scratch_shapes=[
                pltpu.VMEM(shape, jnp.bfloat16),
                pltpu.SemaphoreType.DMA((LINES,)),
                pltpu.SemaphoreType.DMA,
            ],
        ),
        out_shape=jax.ShapeDtypeStruct(shape, jnp.bfloat16),
        compiler_params=pltpu.CompilerParams(vmem_limit_bytes=PICK_VMEM),
        cost_estimate=pl.CostEstimate(
            flops=PICK_WEIGHT, bytes_accessed=2 * size, transcendentals=0
        ),
        name=name,
    )(*scalars, *operands)


def pick_part(ids, here, part, pieces, rows):
    flat = [array for ps in pieces for array, _ in ps]

    def kernel(ids_ref, here_ref, *refs):
        sources, (out_ref, held, in_sems, out_sem) = refs[:-4], refs[-4:]
        senders, at = [], 0
        for offset, ps in zip(part, pieces):
            z = (here_ref[0] + (offset + STEPS)) & (STEPS - 1)
            senders.append((z, [(sources[at + n], f) for n, (_, f) in enumerate(ps)]))
            at += len(ps)
        copy_blocks(ids_ref, senders, out_ref, held, in_sems, out_sem)

    return pick_call(kernel, (ids, here), flat, len(part) * CAP, rows, "pick_part")


def mix(codes, arrays, weights, bias):
    per_device, taps = weights.shape[:2]
    rows = arrays[0].shape[1]

    def kernel(codes_ref, *refs):
        blocks_refs = refs[: len(arrays)]
        weight_ref, bias_ref, out_ref, held, sems = refs[len(arrays) :]
        j = pl.program_id(0)

        def fetch(which, into):
            def choose(code, k, first, last):
                if last - first == 1:
                    pltpu.make_async_copy(
                        blocks_refs[first].at[code & 255],
                        held.at[into, :, k * BLOCK : (k + 1) * BLOCK],
                        sems.at[into],
                    ).start()
                    return
                middle = (first + last) // 2
                low = (code >> 8) < middle
                pl.when(low)(lambda: choose(code, k, first, middle))
                pl.when(jnp.logical_not(low))(lambda: choose(code, k, middle, last))

            for k in range(taps):
                choose(codes_ref[which * taps + k], k, 0, len(blocks_refs))

        @pl.when(j == 0)
        def _():
            fetch(0, 0)

        @pl.when(j + 1 < per_device)
        def _():
            fetch(j + 1, (j + 1) % 2)

        now = j % 2
        pltpu.make_async_copy(held.at[now], held.at[now], sems.at[now]).wait()
        stacked = weight_ref[0].reshape(taps * BLOCK, BLOCK)
        mixed = jnp.dot(held[now], stacked, preferred_element_type=jnp.float32)
        result = mixed + bias_ref[0]
        out_ref[...] = jnp.clip(result, 0.0, CLAMP_TOP).astype(jnp.bfloat16)

    return pl.pallas_call(
        kernel,
        grid_spec=pltpu.PrefetchScalarGridSpec(
            num_scalar_prefetch=1,
            grid=(per_device,),
            in_specs=[pl.BlockSpec(memory_space=pltpu.HBM)] * len(arrays)
            + [
                pl.BlockSpec((1, taps, BLOCK, BLOCK), lambda j, s: (j, 0, 0, 0)),
                pl.BlockSpec((1, 1, BLOCK), lambda j, s: (j, 0, 0)),
            ],
            out_specs=pl.BlockSpec((rows, BLOCK), lambda j, s: (0, j)),
            scratch_shapes=[
                pltpu.VMEM((2, rows, taps * BLOCK), jnp.bfloat16),
                pltpu.SemaphoreType.DMA((2,)),
            ],
        ),
        out_shape=jax.ShapeDtypeStruct((rows, per_device * BLOCK), jnp.bfloat16),
        compiler_params=pltpu.CompilerParams(vmem_limit_bytes=MIX_VMEM),
        cost_estimate=pl.CostEstimate(
            flops=2 * rows * per_device * taps * BLOCK * BLOCK,
            bytes_accessed=per_device * taps * (rows + BLOCK) * BLOCK * 2,
            transcendentals=0,
        ),
        name="mix",
    )(codes, *arrays, weights, bias.reshape(per_device, 1, BLOCK))


def shifted(value, axis, by):
    count = lax.axis_size(axis)
    return lax.ppermute(value, axis, [(i, (i + by) % count) for i in range(count)])


def over_lines(outgoing):
    incoming = lax.all_to_all(outgoing, "y", 0, 0, tiled=True)
    return incoming.reshape((-1,) + incoming.shape[2:])


def part_codes(slots, here):
    line, z, c = slots >> 5, (slots >> 1) & (STEPS - 1), slots & 1
    offset = (z - here) & (STEPS - 1)
    codes = jnp.zeros_like(slots)
    for p, part in enumerate(PARTS):
        for i, o in enumerate(part):
            code = p * 256 + line * (len(part) * CAP) + i * CAP + c
            codes = jnp.where(offset == o % STEPS, code, codes)
    return codes


def body(layer_input, weight_blocks, neuron_bias, block_slots, send_lists):
    samples, weights, bias = layer_input[0], weight_blocks[0], neuron_bias[0]
    slots = block_slots.reshape(-1)
    here = lax.axis_index("z").astype(jnp.int32)
    lists = send_lists.reshape(LINES, STEPS, CAP).transpose(1, 0, 2)

    held = {0: [(samples, 0)]}
    up = down = samples
    picked, arrived = [], []

    def pick_next():
        part = PARTS[len(picked)]
        pieces = [held[o] for o in part]
        picked.append(pick_part(ids, here.reshape(1), part, pieces, samples.shape[0]))

    def send_next():
        arrived.append(over_lines(picked[len(arrived)]))

    ids = lax.all_to_all(lists, "z", 0, 0, tiled=True).reshape(-1)
    last = STEPS // 2
    half = samples.shape[0] // 32 * 16
    waiting = []
    for step in range(1, last + 1):
        if step == IDS_STEP:
            ids, up, down = lax.optimization_barrier((ids, up, down))
        for ready, index in waiting:
            if step == ready + 2:
                picked[index], up, down = lax.optimization_barrier(
                    (picked[index], up, down)
                )
                send_next()
            if step == HAVE[index]:
                arrived[index], up, down = lax.optimization_barrier(
                    (arrived[index], up, down)
                )
        if step < last:
            up, down = shifted(up, "z", 1), shifted(down, "z", -1)
            held[-step], held[step] = [(up, 0)], [(down, 0)]
        else:
            up, down = shifted(up[:half], "z", 1), shifted(down[half:], "z", -1)
            held[step] = [(up, 0), (down, half)]
        if all(o in held for o in PARTS[len(picked)]):
            waiting.append((step, len(picked)))
            pick_next()
    send_next()

    out = mix(part_codes(slots, here), arrived, weights, bias)
    return shifted(out, "segment", 1)[None]


def solution(mesh):
    segments, row = mesh.devices.shape
    split = Mesh(
        mesh.devices.reshape(segments, row // STEPS, STEPS), ("segment", "y", "z")
    )
    row = ("y", "z")
    placed = (
        P("segment", None, row),
        P("segment", row, None, None, None),
        P("segment", row),
        P("segment", row, None),
        P("segment", row, None, None),
    )
    return jax.shard_map(
        body,
        mesh=split,
        in_specs=placed,
        out_specs=P("segment", None, row),
        check_vma=False,
    )
```

```python
import jax
import jax.numpy as jnp
from jax import lax
from jax.experimental import pallas as pl
from jax.experimental.pallas import tpu as pltpu
from jax.sharding import Mesh, PartitionSpec as P

CLAMP_TOP = 3.0
LINES = 4
STEPS = 16
GROUP = 4
Z = ("far", "near")
CAP = 2
BLOCK = 128
PICK_VMEM = 24 * 2**20
MIX_VMEM = 58 * 2**20
PICK_WEIGHT = 12 * 10**9
AFTER = (2,)
HAVE = (5, 8, 9, 9)
PARTS = (
    (0, -1, 1),
    (-2, 2, -3, 3),
    (-4, 4, -5, 5),
    (-6, 6, -7, 7, 8),
)


def copy_blocks(ids_ref, senders, out_ref, held, in_sems, out_sem):
    for y in range(LINES):
        for i, (z, pieces) in enumerate(senders):
            for c in range(CAP):
                block = ids_ref[(z * LINES + y) * CAP + c] & 7
                columns = pl.ds(pl.multiple_of(block * BLOCK, BLOCK), BLOCK)
                for ref, first in pieces:
                    rows = pl.ds(first, ref.shape[0])
                    pltpu.make_async_copy(
                        ref.at[:, columns], held.at[y, i * CAP + c, rows], in_sems.at[y]
                    ).start()
    for y in range(LINES):
        pltpu.make_async_copy(held.at[y], held.at[y], in_sems.at[y]).wait()
        pltpu.make_async_copy(held.at[y], out_ref.at[y], out_sem).start()
    pltpu.make_async_copy(held, held, out_sem).wait()


def pick_call(kernel, scalars, operands, count, rows, name):
    shape = (LINES, count, rows, BLOCK)
    size = LINES * count * rows * BLOCK * 2
    return pl.pallas_call(
        kernel,
        grid_spec=pltpu.PrefetchScalarGridSpec(
            num_scalar_prefetch=len(scalars),
            grid=(1,),
            in_specs=[pl.BlockSpec(memory_space=pltpu.HBM)] * len(operands),
            out_specs=pl.BlockSpec(memory_space=pltpu.HBM),
            scratch_shapes=[
                pltpu.VMEM(shape, jnp.bfloat16),
                pltpu.SemaphoreType.DMA((LINES,)),
                pltpu.SemaphoreType.DMA,
            ],
        ),
        out_shape=jax.ShapeDtypeStruct(shape, jnp.bfloat16),
        compiler_params=pltpu.CompilerParams(vmem_limit_bytes=PICK_VMEM),
        cost_estimate=pl.CostEstimate(
            flops=PICK_WEIGHT, bytes_accessed=2 * size, transcendentals=0
        ),
        name=name,
    )(*scalars, *operands)


def pick_part(ids, here, part, pieces, rows):
    flat = [array for ps in pieces for array, _ in ps]

    def kernel(ids_ref, here_ref, *refs):
        sources, (out_ref, held, in_sems, out_sem) = refs[:-4], refs[-4:]
        senders, at = [], 0
        for offset, ps in zip(part, pieces):
            z = (here_ref[0] + (offset + STEPS)) & (STEPS - 1)
            senders.append((z, [(sources[at + n], f) for n, (_, f) in enumerate(ps)]))
            at += len(ps)
        copy_blocks(ids_ref, senders, out_ref, held, in_sems, out_sem)

    return pick_call(kernel, (ids, here), flat, len(part) * CAP, rows, "pick_part")


def mix(codes, arrays, weights, bias):
    per_device, taps = weights.shape[:2]
    rows = arrays[0].shape[1]

    def kernel(codes_ref, *refs):
        blocks_refs = refs[: len(arrays)]
        weight_ref, bias_ref, out_ref, held, sems = refs[len(arrays) :]
        j = pl.program_id(0)

        def fetch(which, into):
            def choose(code, k, first, last):
                if last - first == 1:
                    pltpu.make_async_copy(
                        blocks_refs[first].at[code & 255],
                        held.at[into, :, k * BLOCK : (k + 1) * BLOCK],
                        sems.at[into],
                    ).start()
                    return
                middle = (first + last) // 2
                low = (code >> 8) < middle
                pl.when(low)(lambda: choose(code, k, first, middle))
                pl.when(jnp.logical_not(low))(lambda: choose(code, k, middle, last))

            for k in range(taps):
                choose(codes_ref[which * taps + k], k, 0, len(blocks_refs))

        @pl.when(j == 0)
        def _():
            fetch(0, 0)

        @pl.when(j + 1 < per_device)
        def _():
            fetch(j + 1, (j + 1) % 2)

        now = j % 2
        pltpu.make_async_copy(held.at[now], held.at[now], sems.at[now]).wait()
        stacked = weight_ref[0].reshape(taps * BLOCK, BLOCK)
        mixed = jnp.dot(held[now], stacked, preferred_element_type=jnp.float32)
        result = mixed + bias_ref[0]
        out_ref[...] = jnp.clip(result, 0.0, CLAMP_TOP).astype(jnp.bfloat16)

    return pl.pallas_call(
        kernel,
        grid_spec=pltpu.PrefetchScalarGridSpec(
            num_scalar_prefetch=1,
            grid=(per_device,),
            in_specs=[pl.BlockSpec(memory_space=pltpu.HBM)] * len(arrays)
            + [
                pl.BlockSpec((1, taps, BLOCK, BLOCK), lambda j, s: (j, 0, 0, 0)),
                pl.BlockSpec((1, 1, BLOCK), lambda j, s: (j, 0, 0)),
            ],
            out_specs=pl.BlockSpec((rows, BLOCK), lambda j, s: (0, j)),
            scratch_shapes=[
                pltpu.VMEM((2, rows, taps * BLOCK), jnp.bfloat16),
                pltpu.SemaphoreType.DMA((2,)),
            ],
        ),
        out_shape=jax.ShapeDtypeStruct((rows, per_device * BLOCK), jnp.bfloat16),
        compiler_params=pltpu.CompilerParams(vmem_limit_bytes=MIX_VMEM),
        cost_estimate=pl.CostEstimate(
            flops=2 * rows * per_device * taps * BLOCK * BLOCK,
            bytes_accessed=per_device * taps * (rows + BLOCK) * BLOCK * 2,
            transcendentals=0,
        ),
        name="mix",
    )(codes, *arrays, weights, bias.reshape(per_device, 1, BLOCK))


def shifted(value, axis, by):
    count = lax.axis_size(axis)
    return lax.ppermute(value, axis, [(i, (i + by) % count) for i in range(count)])


def over_lines(outgoing):
    incoming = lax.all_to_all(outgoing, "y", 0, 0, tiled=True)
    return incoming.reshape((-1,) + incoming.shape[2:])


def part_codes(slots, here):
    line, z, c = slots >> 5, (slots >> 1) & (STEPS - 1), slots & 1
    offset = (z - here) & (STEPS - 1)
    codes = jnp.zeros_like(slots)
    for p, part in enumerate(PARTS):
        for i, o in enumerate(part):
            code = p * 256 + line * (len(part) * CAP) + i * CAP + c
            codes = jnp.where(offset == o % STEPS, code, codes)
    return codes


def body(layer_input, weight_blocks, neuron_bias, block_slots, send_lists):
    samples, weights, bias = layer_input[0], weight_blocks[0], neuron_bias[0]
    slots = block_slots.reshape(-1)
    here = lax.axis_index(Z).astype(jnp.int32)
    lists = send_lists.reshape(LINES, GROUP, GROUP, CAP).transpose(2, 1, 0, 3)

    held = {0: [(samples, 0)]}
    up = down = samples
    picked, arrived = [], []

    def pick_next():
        part = PARTS[len(picked)]
        pieces = [held[o] for o in part]
        picked.append(pick_part(ids, here.reshape(1), part, pieces, samples.shape[0]))

    def send_next():
        arrived.append(over_lines(picked[len(arrived)]))

    near = lax.all_to_all(lists, "near", 0, 0, tiled=True)
    last = STEPS // 2
    half = samples.shape[0] // 32 * 16
    ready = []
    for step in range(1, last + 1):
        if step == 2:
            near, up, down = lax.optimization_barrier((near, up, down))
            far = near.transpose(1, 0, 2, 3)
            ids = lax.all_to_all(far, "far", 0, 0, tiled=True).reshape(-1)
        for index, done in enumerate(ready):
            if step == done + 2:
                pick_next()
                picked[index], up, down = lax.optimization_barrier(
                    (picked[index], up, down)
                )
                if index in AFTER:
                    picked[index], arrived[-1] = lax.optimization_barrier(
                        (picked[index], arrived[-1])
                    )
                send_next()
            if step == HAVE[index]:
                arrived[index], up, down = lax.optimization_barrier(
                    (arrived[index], up, down)
                )
        if step < last:
            up, down = shifted(up, Z, 1), shifted(down, Z, -1)
            held[-step], held[step] = [(up, 0)], [(down, 0)]
        else:
            up, down = shifted(up[:half], Z, 1), shifted(down[half:], Z, -1)
            held[step] = [(up, 0), (down, half)]
        if all(o in held for o in PARTS[len(ready)]):
            ready.append(step)
    pick_next()
    send_next()

    out = mix(part_codes(slots, here), arrived, weights, bias)
    return shifted(out, "segment", 1)[None]


def solution(mesh):
    segments, row = mesh.devices.shape
    split = Mesh(
        mesh.devices.reshape(segments, row // STEPS, GROUP, GROUP), ("segment", "y", *Z)
    )
    row = ("y", *Z)
    placed = (
        P("segment", None, row),
        P("segment", row, None, None, None),
        P("segment", row),
        P("segment", row, None),
        P("segment", row, None, None),
    )
    return jax.shard_map(
        body,
        mesh=split,
        in_specs=placed,
        out_specs=P("segment", None, row),
        check_vma=False,
    )
```

```python
import jax
import jax.numpy as jnp
from jax import lax
from jax.experimental import pallas as pl
from jax.experimental.pallas import tpu as pltpu
from jax.sharding import Mesh, PartitionSpec as P

CLAMP_TOP = 3.0
LINES = 4
STEPS = 16
GROUP = 4
Z = ("far", "near")
CAP = 2
BLOCK = 128
PICK_VMEM = 24 * 2**20
MIX_VMEM = 50 * 2**20
PICK_WEIGHT = 12 * 10**9
AFTER = (2,)
HAVE = (6, 9, 9, 9)
PARTS = (
    (0, -1, 1, -2, 2),
    (-3, 3, -4, 4),
    (-5, 5, -6, 6),
    (-7, 7, 8),
)


def copy_blocks(ids_ref, senders, out_ref, held, in_sems, out_sem):
    for y in range(LINES):
        for i, (z, pieces) in enumerate(senders):
            for c in range(CAP):
                block = ids_ref[(z * LINES + y) * CAP + c] & 7
                columns = pl.ds(pl.multiple_of(block * BLOCK, BLOCK), BLOCK)
                for ref, first in pieces:
                    rows = pl.ds(first, ref.shape[0])
                    pltpu.make_async_copy(
                        ref.at[:, columns], held.at[y, i * CAP + c, rows], in_sems.at[y]
                    ).start()
    for y in range(LINES):
        pltpu.make_async_copy(held.at[y], held.at[y], in_sems.at[y]).wait()
        pltpu.make_async_copy(held.at[y], out_ref.at[y], out_sem).start()
    pltpu.make_async_copy(held, held, out_sem).wait()


def pick_call(kernel, scalars, operands, count, rows, name):
    shape = (LINES, count, rows, BLOCK)
    size = LINES * count * rows * BLOCK * 2
    return pl.pallas_call(
        kernel,
        grid_spec=pltpu.PrefetchScalarGridSpec(
            num_scalar_prefetch=len(scalars),
            grid=(1,),
            in_specs=[pl.BlockSpec(memory_space=pltpu.HBM)] * len(operands),
            out_specs=pl.BlockSpec(memory_space=pltpu.HBM),
            scratch_shapes=[
                pltpu.VMEM(shape, jnp.bfloat16),
                pltpu.SemaphoreType.DMA((LINES,)),
                pltpu.SemaphoreType.DMA,
            ],
        ),
        out_shape=jax.ShapeDtypeStruct(shape, jnp.bfloat16),
        compiler_params=pltpu.CompilerParams(vmem_limit_bytes=PICK_VMEM),
        cost_estimate=pl.CostEstimate(
            flops=PICK_WEIGHT, bytes_accessed=2 * size, transcendentals=0
        ),
        name=name,
    )(*scalars, *operands)


def pick_part(ids, here, part, pieces, rows):
    flat = [array for ps in pieces for array, _ in ps]

    def kernel(ids_ref, here_ref, *refs):
        sources, (out_ref, held, in_sems, out_sem) = refs[:-4], refs[-4:]
        senders, at = [], 0
        for offset, ps in zip(part, pieces):
            z = (here_ref[0] + (offset + STEPS)) & (STEPS - 1)
            senders.append((z, [(sources[at + n], f) for n, (_, f) in enumerate(ps)]))
            at += len(ps)
        copy_blocks(ids_ref, senders, out_ref, held, in_sems, out_sem)

    return pick_call(kernel, (ids, here), flat, len(part) * CAP, rows, "pick_part")


def mix(codes, arrays, weights, bias, first, rows):
    per_device, taps = weights.shape[:2]
    total = sum(array.shape[0] for array in arrays)

    def kernel(codes_ref, *refs):
        blocks_refs = refs[: len(arrays)]
        weight_ref, bias_ref, out_ref, held, sem = refs[len(arrays) :]
        j = pl.program_id(0)

        @pl.when(j == 0)
        def _():
            at = 0
            for ref in blocks_refs:
                pltpu.make_async_copy(
                    ref.at[:, first : first + rows],
                    held.at[at : at + ref.shape[0]],
                    sem,
                ).start()
                at += ref.shape[0]
            pltpu.make_async_copy(held, held, sem).wait()

        blocks = [held[codes_ref[j * taps + k]] for k in range(taps)]
        stacked = weight_ref[0].reshape(taps * BLOCK, BLOCK)
        mixed = jnp.dot(
            jnp.concatenate(blocks, axis=1), stacked, preferred_element_type=jnp.float32
        )
        result = mixed + bias_ref[0]
        out_ref[...] = jnp.clip(result, 0.0, CLAMP_TOP).astype(jnp.bfloat16)

    return pl.pallas_call(
        kernel,
        grid_spec=pltpu.PrefetchScalarGridSpec(
            num_scalar_prefetch=1,
            grid=(per_device,),
            in_specs=[pl.BlockSpec(memory_space=pl.ANY)] * len(arrays)
            + [
                pl.BlockSpec((1, taps, BLOCK, BLOCK), lambda j, s: (j, 0, 0, 0)),
                pl.BlockSpec((1, 1, BLOCK), lambda j, s: (j, 0, 0)),
            ],
            out_specs=pl.BlockSpec((rows, BLOCK), lambda j, s: (0, j)),
            scratch_shapes=[
                pltpu.VMEM((total, rows, BLOCK), jnp.bfloat16),
                pltpu.SemaphoreType.DMA,
            ],
        ),
        out_shape=jax.ShapeDtypeStruct((rows, per_device * BLOCK), jnp.bfloat16),
        compiler_params=pltpu.CompilerParams(vmem_limit_bytes=MIX_VMEM),
        cost_estimate=pl.CostEstimate(
            flops=2 * rows * per_device * taps * BLOCK * BLOCK,
            bytes_accessed=(total * rows + per_device * taps * BLOCK) * BLOCK * 2,
            transcendentals=0,
        ),
        name="mix",
    )(codes, *arrays, weights, bias.reshape(per_device, 1, BLOCK))


def shifted(value, axis, by):
    count = lax.axis_size(axis)
    return lax.ppermute(value, axis, [(i, (i + by) % count) for i in range(count)])


def over_lines(outgoing):
    incoming = lax.all_to_all(outgoing, "y", 0, 0, tiled=True)
    return incoming.reshape((-1,) + incoming.shape[2:])


def part_codes(slots, here):
    line, z, c = slots >> 5, (slots >> 1) & (STEPS - 1), slots & 1
    offset = (z - here) & (STEPS - 1)
    codes = jnp.zeros_like(slots)
    base = 0
    for part in PARTS:
        for i, o in enumerate(part):
            code = base + line * (len(part) * CAP) + i * CAP + c
            codes = jnp.where(offset == o % STEPS, code, codes)
        base += LINES * len(part) * CAP
    return codes


def body(layer_input, weight_blocks, neuron_bias, block_slots, send_lists):
    samples, weights, bias = layer_input[0], weight_blocks[0], neuron_bias[0]
    slots = block_slots.reshape(-1)
    here = lax.axis_index(Z).astype(jnp.int32)
    lists = send_lists.reshape(LINES, GROUP, GROUP, CAP).transpose(2, 1, 0, 3)

    held = {0: [(samples, 0)]}
    up = down = samples
    picked, arrived = [], []

    def pick_next():
        part = PARTS[len(picked)]
        pieces = [held[o] for o in part]
        picked.append(pick_part(ids, here.reshape(1), part, pieces, samples.shape[0]))

    def send_next():
        arrived.append(over_lines(picked[len(arrived)]))

    near = lax.all_to_all(lists, "near", 0, 0, tiled=True)
    last = STEPS // 2
    half = samples.shape[0] // 32 * 16
    ready = []
    for step in range(1, last + 1):
        if step == 2:
            near, up, down = lax.optimization_barrier((near, up, down))
            far = near.transpose(1, 0, 2, 3)
            ids = lax.all_to_all(far, "far", 0, 0, tiled=True).reshape(-1)
        for index, done in enumerate(ready):
            if step == done + 2:
                pick_next()
                picked[index], up, down = lax.optimization_barrier(
                    (picked[index], up, down)
                )
                if index in AFTER:
                    picked[index], arrived[-1] = lax.optimization_barrier(
                        (picked[index], arrived[-1])
                    )
                send_next()
            if step == HAVE[index]:
                arrived[index], up, down = lax.optimization_barrier(
                    (arrived[index], up, down)
                )
        if step < last:
            up, down = shifted(up, Z, 1), shifted(down, Z, -1)
            held[-step], held[step] = [(up, 0)], [(down, 0)]
        else:
            up, down = shifted(up[:half], Z, 1), shifted(down[half:], Z, -1)
            held[step] = [(up, 0), (down, half)]
        if all(o in held for o in PARTS[len(ready)]):
            ready.append(step)
    pick_next()
    picked[-1], arrived[-1] = lax.optimization_barrier((picked[-1], arrived[-1]))
    send_next()

    codes = part_codes(slots, here)
    rows = samples.shape[0]
    upper = (rows + 31) // 32 * 16
    outs = [
        shifted(mix(codes, arrived, weights, bias, first, count), "segment", 1)
        for first, count in ((0, upper), (upper, rows - upper))
    ]
    return jnp.concatenate(outs, axis=0)[None]


def solution(mesh):
    segments, row = mesh.devices.shape
    split = Mesh(
        mesh.devices.reshape(segments, row // STEPS, GROUP, GROUP), ("segment", "y", *Z)
    )
    row = ("y", *Z)
    placed = (
        P("segment", None, row),
        P("segment", row, None, None, None),
        P("segment", row),
        P("segment", row, None),
        P("segment", row, None, None),
    )
    return jax.shard_map(
        body,
        mesh=split,
        in_specs=placed,
        out_specs=P("segment", None, row),
        check_vma=False,
    )
```

```python
import jax
import jax.numpy as jnp
from jax import lax
from jax.experimental import pallas as pl
from jax.experimental.pallas import tpu as pltpu
from jax.sharding import Mesh, PartitionSpec as P

CLAMP_TOP = 3.0
LINES = 4
STEPS = 16
GROUP = 4
Z = ("far", "near")
CAP = 2
BLOCK = 128
PICK_VMEM = 24 * 2**20
MIX_VMEM = 50 * 2**20
LATE_VMEM = 50 * 2**20
MIX_WEIGHT = 10**10
PICK_WEIGHT = 12 * 10**9
AFTER = (2,)
HAVE = (5, 8, 9, 9)
PARTS = (
    (0, -1, 1),
    (-2, 2, -3, 3),
    (-4, 4, -5, 5),
    (-6, 6, -7, 7, 8),
)


def copy_blocks(ids_ref, senders, out_ref, held, in_sems, out_sem):
    for y in range(LINES):
        for i, (z, pieces) in enumerate(senders):
            for c in range(CAP):
                block = ids_ref[(z * LINES + y) * CAP + c] & 7
                columns = pl.ds(pl.multiple_of(block * BLOCK, BLOCK), BLOCK)
                for ref, first in pieces:
                    rows = pl.ds(first, ref.shape[0])
                    pltpu.make_async_copy(
                        ref.at[:, columns], held.at[y, i * CAP + c, rows], in_sems.at[y]
                    ).start()
    for y in range(LINES):
        pltpu.make_async_copy(held.at[y], held.at[y], in_sems.at[y]).wait()
        pltpu.make_async_copy(held.at[y], out_ref.at[y], out_sem).start()
    pltpu.make_async_copy(held, held, out_sem).wait()


def pick_call(kernel, scalars, operands, count, rows, name):
    shape = (LINES, count, rows, BLOCK)
    size = LINES * count * rows * BLOCK * 2
    return pl.pallas_call(
        kernel,
        grid_spec=pltpu.PrefetchScalarGridSpec(
            num_scalar_prefetch=len(scalars),
            grid=(1,),
            in_specs=[pl.BlockSpec(memory_space=pltpu.HBM)] * len(operands),
            out_specs=pl.BlockSpec(memory_space=pltpu.HBM),
            scratch_shapes=[
                pltpu.VMEM(shape, jnp.bfloat16),
                pltpu.SemaphoreType.DMA((LINES,)),
                pltpu.SemaphoreType.DMA,
            ],
        ),
        out_shape=jax.ShapeDtypeStruct(shape, jnp.bfloat16),
        compiler_params=pltpu.CompilerParams(vmem_limit_bytes=PICK_VMEM),
        cost_estimate=pl.CostEstimate(
            flops=PICK_WEIGHT, bytes_accessed=2 * size, transcendentals=0
        ),
        name=name,
    )(*scalars, *operands)


def pick_part(ids, here, part, pieces, rows):
    flat = [array for ps in pieces for array, _ in ps]

    def kernel(ids_ref, here_ref, *refs):
        sources, (out_ref, held, in_sems, out_sem) = refs[:-4], refs[-4:]
        senders, at = [], 0
        for offset, ps in zip(part, pieces):
            z = (here_ref[0] + (offset + STEPS)) & (STEPS - 1)
            senders.append((z, [(sources[at + n], f) for n, (_, f) in enumerate(ps)]))
            at += len(ps)
        copy_blocks(ids_ref, senders, out_ref, held, in_sems, out_sem)

    return pick_call(kernel, (ids, here), flat, len(part) * CAP, rows, "pick_part")


def mix_early(codes, arrays, weights):
    per_device, taps = weights.shape[:2]
    rows = arrays[0].shape[1]
    total = sum(array.shape[0] for array in arrays)

    def kernel(codes_ref, *refs):
        blocks_refs = refs[: len(arrays)]
        weight_ref, out_ref, held, sem = refs[len(arrays) :]
        j = pl.program_id(0)
        here = held.at[pl.ds(0, total)]

        @pl.when(j == 0)
        def _():
            at = 0
            for ref in blocks_refs:
                pltpu.make_async_copy(ref, held.at[pl.ds(at, ref.shape[0])], sem).start()
                at += ref.shape[0]
            held[total] = jnp.zeros((rows, BLOCK), jnp.bfloat16)
            pltpu.make_async_copy(here, here, sem).wait()

        blocks = [
            held[jnp.minimum(codes_ref[j * taps + k], total)] for k in range(taps)
        ]
        out_ref[...] = jnp.dot(
            jnp.concatenate(blocks, axis=1),
            weight_ref[0].reshape(taps * BLOCK, BLOCK),
            preferred_element_type=jnp.float32,
        )

    return pl.pallas_call(
        kernel,
        grid_spec=pltpu.PrefetchScalarGridSpec(
            num_scalar_prefetch=1,
            grid=(per_device,),
            in_specs=[pl.BlockSpec(memory_space=pl.ANY)] * len(arrays)
            + [pl.BlockSpec((1, taps, BLOCK, BLOCK), lambda j, s: (j, 0, 0, 0))],
            out_specs=pl.BlockSpec((rows, BLOCK), lambda j, s: (0, j)),
            scratch_shapes=[
                pltpu.VMEM((total + 1, rows, BLOCK), jnp.bfloat16),
                pltpu.SemaphoreType.DMA,
            ],
        ),
        out_shape=jax.ShapeDtypeStruct((rows, per_device * BLOCK), jnp.float32),
        compiler_params=pltpu.CompilerParams(vmem_limit_bytes=MIX_VMEM),
        cost_estimate=pl.CostEstimate(
            flops=MIX_WEIGHT,
            bytes_accessed=(total * rows + per_device * taps * BLOCK) * BLOCK * 2,
            transcendentals=0,
        ),
        name="mix_early",
    )(codes, *arrays, weights)


def mix_late(codes, early, array, base, weights, bias, first, count):
    taps = weights.shape[1]
    size, rows = array.shape[:2]

    def kernel(codes_ref, early_ref, blocks_ref, weight_ref, bias_ref, out_ref, total):
        j = pl.program_id(0) + first
        total[...] = early_ref[...] + bias_ref[0]
        for k in range(taps):
            place = codes_ref[j * taps + k] - base

            @pl.when(place >= 0)
            def _(k=k, place=place):
                total[...] += jnp.dot(
                    blocks_ref[place],
                    weight_ref[0, k],
                    preferred_element_type=jnp.float32,
                )

        out_ref[...] = jnp.clip(total[...], 0.0, CLAMP_TOP).astype(jnp.bfloat16)

    return pl.pallas_call(
        kernel,
        grid_spec=pltpu.PrefetchScalarGridSpec(
            num_scalar_prefetch=1,
            grid=(count,),
            in_specs=[
                pl.BlockSpec((rows, BLOCK), lambda j, s: (0, j + first)),
                pl.BlockSpec((size, rows, BLOCK), lambda j, s: (0, 0, 0)),
                pl.BlockSpec(
                    (1, taps, BLOCK, BLOCK), lambda j, s: (j + first, 0, 0, 0)
                ),
                pl.BlockSpec((1, 1, BLOCK), lambda j, s: (j + first, 0, 0)),
            ],
            out_specs=pl.BlockSpec((rows, BLOCK), lambda j, s: (0, j)),
            scratch_shapes=[pltpu.VMEM((rows, BLOCK), jnp.float32)],
        ),
        out_shape=jax.ShapeDtypeStruct((rows, count * BLOCK), jnp.bfloat16),
        compiler_params=pltpu.CompilerParams(vmem_limit_bytes=LATE_VMEM),
        cost_estimate=pl.CostEstimate(
            flops=2 * rows * count * taps * BLOCK * BLOCK,
            bytes_accessed=(size * rows + count * taps * BLOCK) * BLOCK * 2,
            transcendentals=0,
        ),
        name="mix_late",
    )(codes, early, array, weights, bias.reshape(-1, 1, BLOCK))


def shifted(value, axis, by):
    count = lax.axis_size(axis)
    return lax.ppermute(value, axis, [(i, (i + by) % count) for i in range(count)])


def over_lines(outgoing):
    incoming = lax.all_to_all(outgoing, "y", 0, 0, tiled=True)
    return incoming.reshape((-1,) + incoming.shape[2:])


def part_codes(slots, here):
    line, z, c = slots >> 5, (slots >> 1) & (STEPS - 1), slots & 1
    offset = (z - here) & (STEPS - 1)
    codes = jnp.zeros_like(slots)
    base = 0
    for part in PARTS:
        for i, o in enumerate(part):
            code = base + line * (len(part) * CAP) + i * CAP + c
            codes = jnp.where(offset == o % STEPS, code, codes)
        base += LINES * len(part) * CAP
    return codes


def body(layer_input, weight_blocks, neuron_bias, block_slots, send_lists):
    samples, weights, bias = layer_input[0], weight_blocks[0], neuron_bias[0]
    slots = block_slots.reshape(-1)
    here = lax.axis_index(Z).astype(jnp.int32)
    lists = send_lists.reshape(LINES, GROUP, GROUP, CAP).transpose(2, 1, 0, 3)

    held = {0: [(samples, 0)]}
    up = down = samples
    picked, arrived = [], []

    def pick_next():
        part = PARTS[len(picked)]
        pieces = [held[o] for o in part]
        picked.append(pick_part(ids, here.reshape(1), part, pieces, samples.shape[0]))

    def send_next():
        arrived.append(over_lines(picked[len(arrived)]))

    near = lax.all_to_all(lists, "near", 0, 0, tiled=True)
    last = STEPS // 2
    half = samples.shape[0] // 32 * 16
    ready = []
    for step in range(1, last + 1):
        if step == 2:
            near, up, down = lax.optimization_barrier((near, up, down))
            far = near.transpose(1, 0, 2, 3)
            ids = lax.all_to_all(far, "far", 0, 0, tiled=True).reshape(-1)
        for index, done in enumerate(ready):
            if step == done + 2:
                pick_next()
                picked[index], up, down = lax.optimization_barrier(
                    (picked[index], up, down)
                )
                if index in AFTER:
                    picked[index], arrived[-1] = lax.optimization_barrier(
                        (picked[index], arrived[-1])
                    )
                send_next()
            if step == HAVE[index]:
                arrived[index], up, down = lax.optimization_barrier(
                    (arrived[index], up, down)
                )
        if step < last:
            up, down = shifted(up, Z, 1), shifted(down, Z, -1)
            held[-step], held[step] = [(up, 0)], [(down, 0)]
        else:
            up, down = shifted(up[:half], Z, 1), shifted(down[half:], Z, -1)
            held[step] = [(up, 0), (down, half)]
        if all(o in held for o in PARTS[len(ready)]):
            ready.append(step)
    pick_next()
    send_next()

    codes = part_codes(slots, here)
    early = mix_early(codes, arrived[:-1], weights)
    base = sum(array.shape[0] for array in arrived[:-1])
    cut = weights.shape[0] * 5 // 8
    outs = [
        mix_late(codes, early, arrived[-1], base, weights, bias, first, last - first)
        for first, last in ((0, cut), (cut, weights.shape[0]))
    ]
    outs = [shifted(out, "segment", 1) for out in outs]
    return jnp.concatenate(outs, axis=1)[None]


def solution(mesh):
    segments, row = mesh.devices.shape
    split = Mesh(
        mesh.devices.reshape(segments, row // STEPS, GROUP, GROUP), ("segment", "y", *Z)
    )
    row = ("y", *Z)
    placed = (
        P("segment", None, row),
        P("segment", row, None, None, None),
        P("segment", row),
        P("segment", row, None),
        P("segment", row, None, None),
    )
    return jax.shard_map(
        body,
        mesh=split,
        in_specs=placed,
        out_specs=P("segment", None, row),
        check_vma=False,
    )
```

```python
import jax
import jax.numpy as jnp
from jax import lax
from jax.experimental import pallas as pl
from jax.experimental.pallas import tpu as pltpu
from jax.sharding import Mesh, PartitionSpec as P

CLAMP_TOP = 3.0
LINES = 4
STEPS = 16
GROUP = 4
Z = ("far", "near")
CAP = 2
BLOCK = 128
PICK_VMEM = 24 * 2**20
MIX_VMEM = 50 * 2**20
LATE_VMEM = 50 * 2**20
MIX_WEIGHT = 10**10
PICK_WEIGHT = 12 * 10**9
AFTER = (2,)
HAVE = (5, 8, 9, 9)
PARTS = (
    (0, -1, 1),
    (-2, 2, -3, 3),
    (-4, 4, -5, 5),
    (-6, 6, -7, 7, 8),
)


def copy_blocks(ids_ref, senders, out_ref, held, in_sems, out_sem):
    for y in range(LINES):
        for i, (z, pieces) in enumerate(senders):
            for c in range(CAP):
                block = ids_ref[(z * LINES + y) * CAP + c] & 7
                columns = pl.ds(pl.multiple_of(block * BLOCK, BLOCK), BLOCK)
                for ref, first in pieces:
                    rows = pl.ds(first, ref.shape[0])
                    pltpu.make_async_copy(
                        ref.at[:, columns], held.at[y, i * CAP + c, rows], in_sems.at[y]
                    ).start()
    for y in range(LINES):
        pltpu.make_async_copy(held.at[y], held.at[y], in_sems.at[y]).wait()
        pltpu.make_async_copy(held.at[y], out_ref.at[y], out_sem).start()
    pltpu.make_async_copy(held, held, out_sem).wait()


def pick_call(kernel, scalars, operands, count, rows, name):
    shape = (LINES, count, rows, BLOCK)
    size = LINES * count * rows * BLOCK * 2
    return pl.pallas_call(
        kernel,
        grid_spec=pltpu.PrefetchScalarGridSpec(
            num_scalar_prefetch=len(scalars),
            grid=(1,),
            in_specs=[pl.BlockSpec(memory_space=pltpu.HBM)] * len(operands),
            out_specs=pl.BlockSpec(memory_space=pltpu.HBM),
            scratch_shapes=[
                pltpu.VMEM(shape, jnp.bfloat16),
                pltpu.SemaphoreType.DMA((LINES,)),
                pltpu.SemaphoreType.DMA,
            ],
        ),
        out_shape=jax.ShapeDtypeStruct(shape, jnp.bfloat16),
        compiler_params=pltpu.CompilerParams(vmem_limit_bytes=PICK_VMEM),
        cost_estimate=pl.CostEstimate(
            flops=PICK_WEIGHT, bytes_accessed=2 * size, transcendentals=0
        ),
        name=name,
    )(*scalars, *operands)


def pick_part(ids, here, part, pieces, rows):
    flat = [array for ps in pieces for array, _ in ps]

    def kernel(ids_ref, here_ref, *refs):
        sources, (out_ref, held, in_sems, out_sem) = refs[:-4], refs[-4:]
        senders, at = [], 0
        for offset, ps in zip(part, pieces):
            z = (here_ref[0] + (offset + STEPS)) & (STEPS - 1)
            senders.append((z, [(sources[at + n], f) for n, (_, f) in enumerate(ps)]))
            at += len(ps)
        copy_blocks(ids_ref, senders, out_ref, held, in_sems, out_sem)

    return pick_call(kernel, (ids, here), flat, len(part) * CAP, rows, "pick_part")


def mix_early(codes, arrays, weights):
    per_device, taps = weights.shape[:2]
    rows = arrays[0].shape[1]
    total = sum(array.shape[0] for array in arrays)

    def kernel(codes_ref, *refs):
        blocks_refs = refs[: len(arrays)]
        weight_ref, out_ref, held, sem = refs[len(arrays) :]
        j = pl.program_id(0)
        here = held.at[pl.ds(0, total)]

        @pl.when(j == 0)
        def _():
            at = 0
            for ref in blocks_refs:
                pltpu.make_async_copy(ref, held.at[pl.ds(at, ref.shape[0])], sem).start()
                at += ref.shape[0]
            held[total] = jnp.zeros((rows, BLOCK), jnp.bfloat16)
            pltpu.make_async_copy(here, here, sem).wait()

        blocks = [
            held[jnp.minimum(codes_ref[j * taps + k], total)] for k in range(taps)
        ]
        out_ref[...] = jnp.dot(
            jnp.concatenate(blocks, axis=1),
            weight_ref[0].reshape(taps * BLOCK, BLOCK),
            preferred_element_type=jnp.float32,
        )

    return pl.pallas_call(
        kernel,
        grid_spec=pltpu.PrefetchScalarGridSpec(
            num_scalar_prefetch=1,
            grid=(per_device,),
            in_specs=[pl.BlockSpec(memory_space=pl.ANY)] * len(arrays)
            + [pl.BlockSpec((1, taps, BLOCK, BLOCK), lambda j, s: (j, 0, 0, 0))],
            out_specs=pl.BlockSpec((rows, BLOCK), lambda j, s: (0, j)),
            scratch_shapes=[
                pltpu.VMEM((total + 1, rows, BLOCK), jnp.bfloat16),
                pltpu.SemaphoreType.DMA,
            ],
        ),
        out_shape=jax.ShapeDtypeStruct((rows, per_device * BLOCK), jnp.float32),
        compiler_params=pltpu.CompilerParams(vmem_limit_bytes=MIX_VMEM),
        cost_estimate=pl.CostEstimate(
            flops=MIX_WEIGHT,
            bytes_accessed=(total * rows + per_device * taps * BLOCK) * BLOCK * 2,
            transcendentals=0,
        ),
        name="mix_early",
    )(codes, *arrays, weights)


def late_first(codes, base, per_device):
    places = codes.reshape(per_device, -1) - base
    taps = places.shape[1]
    late = places >= 0
    tap = jnp.arange(taps, dtype=jnp.int32)
    before = (tap[None, :, None] > tap[None, None, :]) & late[:, None, :]
    rank = jnp.sum(before.astype(jnp.int32), axis=2)
    chosen = late[:, None, :] & (rank[:, None, :] == tap[None, :, None])
    place = jnp.sum(jnp.where(chosen, places[:, None, :], 0), axis=2)
    which = jnp.sum(jnp.where(chosen, tap[None, None, :], 0), axis=2)
    count = jnp.sum(late.astype(jnp.int32), axis=1)
    return place.reshape(-1), which.reshape(-1), count


def mix_late(late, early, array, weights, bias, first, count):
    taps = weights.shape[1]
    size, rows = array.shape[:2]
    step = 4

    def kernel(
        place_ref, which_ref, count_ref, early_ref, blocks_ref, weight_ref, bias_ref, out_ref, total
    ):
        j = pl.program_id(0) + first
        total[...] = early_ref[...] + bias_ref[0]
        here = count_ref[j]
        for k in range(0, taps, step):

            @pl.when(k < here)
            def _(k=k):
                inputs, stack = [], []
                for i in range(k, k + step):
                    kept = jnp.where(i < here, 1.0, 0.0).astype(jnp.bfloat16)
                    inputs.append(blocks_ref[place_ref[j * taps + i]] * kept)
                    stack.append(weight_ref[0, which_ref[j * taps + i]])
                total[...] += jnp.dot(
                    jnp.concatenate(inputs, axis=1),
                    jnp.concatenate(stack, axis=0),
                    preferred_element_type=jnp.float32,
                )

        out_ref[...] = jnp.clip(total[...], 0.0, CLAMP_TOP).astype(jnp.bfloat16)

    return pl.pallas_call(
        kernel,
        grid_spec=pltpu.PrefetchScalarGridSpec(
            num_scalar_prefetch=3,
            grid=(count,),
            in_specs=[
                pl.BlockSpec((rows, BLOCK), lambda j, *s: (0, j + first)),
                pl.BlockSpec((size, rows, BLOCK), lambda j, *s: (0, 0, 0)),
                pl.BlockSpec(
                    (1, taps, BLOCK, BLOCK), lambda j, *s: (j + first, 0, 0, 0)
                ),
                pl.BlockSpec((1, 1, BLOCK), lambda j, *s: (j + first, 0, 0)),
            ],
            out_specs=pl.BlockSpec((rows, BLOCK), lambda j, *s: (0, j)),
            scratch_shapes=[pltpu.VMEM((rows, BLOCK), jnp.float32)],
        ),
        out_shape=jax.ShapeDtypeStruct((rows, count * BLOCK), jnp.bfloat16),
        compiler_params=pltpu.CompilerParams(vmem_limit_bytes=LATE_VMEM),
        cost_estimate=pl.CostEstimate(
            flops=2 * rows * count * taps * BLOCK * BLOCK,
            bytes_accessed=(size * rows + count * taps * BLOCK) * BLOCK * 2,
            transcendentals=0,
        ),
        name="mix_late",
    )(*late, early, array, weights, bias.reshape(-1, 1, BLOCK))


def shifted(value, axis, by):
    count = lax.axis_size(axis)
    return lax.ppermute(value, axis, [(i, (i + by) % count) for i in range(count)])


def over_lines(outgoing):
    incoming = lax.all_to_all(outgoing, "y", 0, 0, tiled=True)
    return incoming.reshape((-1,) + incoming.shape[2:])


def part_codes(slots, here):
    line, z, c = slots >> 5, (slots >> 1) & (STEPS - 1), slots & 1
    offset = (z - here) & (STEPS - 1)
    codes = jnp.zeros_like(slots)
    base = 0
    for part in PARTS:
        for i, o in enumerate(part):
            code = base + line * (len(part) * CAP) + i * CAP + c
            codes = jnp.where(offset == o % STEPS, code, codes)
        base += LINES * len(part) * CAP
    return codes


def body(layer_input, weight_blocks, neuron_bias, block_slots, send_lists):
    samples, weights, bias = layer_input[0], weight_blocks[0], neuron_bias[0]
    slots = block_slots.reshape(-1)
    here = lax.axis_index(Z).astype(jnp.int32)
    lists = send_lists.reshape(LINES, GROUP, GROUP, CAP).transpose(2, 1, 0, 3)

    held = {0: [(samples, 0)]}
    up = down = samples
    picked, arrived = [], []

    def pick_next():
        part = PARTS[len(picked)]
        pieces = [held[o] for o in part]
        picked.append(pick_part(ids, here.reshape(1), part, pieces, samples.shape[0]))

    def send_next():
        arrived.append(over_lines(picked[len(arrived)]))

    near = lax.all_to_all(lists, "near", 0, 0, tiled=True)
    last = STEPS // 2
    half = samples.shape[0] // 32 * 16
    ready = []
    for step in range(1, last + 1):
        if step == 2:
            near, up, down = lax.optimization_barrier((near, up, down))
            far = near.transpose(1, 0, 2, 3)
            ids = lax.all_to_all(far, "far", 0, 0, tiled=True).reshape(-1)
        for index, done in enumerate(ready):
            if step == done + 2:
                pick_next()
                picked[index], up, down = lax.optimization_barrier(
                    (picked[index], up, down)
                )
                if index in AFTER:
                    picked[index], arrived[-1] = lax.optimization_barrier(
                        (picked[index], arrived[-1])
                    )
                send_next()
            if step == HAVE[index]:
                arrived[index], up, down = lax.optimization_barrier(
                    (arrived[index], up, down)
                )
        if step < last:
            up, down = shifted(up, Z, 1), shifted(down, Z, -1)
            held[-step], held[step] = [(up, 0)], [(down, 0)]
        else:
            up, down = shifted(up[:half], Z, 1), shifted(down[half:], Z, -1)
            held[step] = [(up, 0), (down, half)]
        if all(o in held for o in PARTS[len(ready)]):
            ready.append(step)
    pick_next()
    send_next()

    codes = part_codes(slots, here)
    early = mix_early(codes, arrived[:-1], weights)
    base = sum(array.shape[0] for array in arrived[:-1])
    late = late_first(codes, base, weights.shape[0])
    cut = weights.shape[0] * 5 // 8
    outs = [
        mix_late(late, early, arrived[-1], weights, bias, first, last - first)
        for first, last in ((0, cut), (cut, weights.shape[0]))
    ]
    outs = [shifted(out, "segment", 1) for out in outs]
    return jnp.concatenate(outs, axis=1)[None]


def solution(mesh):
    segments, row = mesh.devices.shape
    split = Mesh(
        mesh.devices.reshape(segments, row // STEPS, GROUP, GROUP), ("segment", "y", *Z)
    )
    row = ("y", *Z)
    placed = (
        P("segment", None, row),
        P("segment", row, None, None, None),
        P("segment", row),
        P("segment", row, None),
        P("segment", row, None, None),
    )
    return jax.shard_map(
        body,
        mesh=split,
        in_specs=placed,
        out_specs=P("segment", None, row),
        check_vma=False,
    )
```

```python
import jax
import jax.numpy as jnp
from jax import lax
from jax.experimental import pallas as pl
from jax.experimental.pallas import tpu as pltpu
from jax.sharding import Mesh, PartitionSpec as P

CLAMP_TOP = 3.0
LINES = 4
STEPS = 16
GROUP = 4
Z = ("far", "near")
CAP = 2
BLOCK = 128
PICK_VMEM = 24 * 2**20
MIX_VMEM = 50 * 2**20
LATE_VMEM = 50 * 2**20
MIX_WEIGHT = 10**10
PICK_WEIGHT = 12 * 10**9
AFTER = (2,)
HAVE = (5, 8, 9, 9)
PARTS = (
    (0, -1, 1),
    (-2, 2, -3, 3),
    (-4, 4, -5, 5),
    (-6, 6, -7, 7, 8),
)


def copy_blocks(ids_ref, senders, out_ref, held, in_sems, out_sem):
    for y in range(LINES):
        for i, (z, pieces) in enumerate(senders):
            for c in range(CAP):
                block = ids_ref[(z * LINES + y) * CAP + c] & 7
                columns = pl.ds(pl.multiple_of(block * BLOCK, BLOCK), BLOCK)
                for ref, first in pieces:
                    rows = pl.ds(first, ref.shape[0])
                    pltpu.make_async_copy(
                        ref.at[:, columns], held.at[y, i * CAP + c, rows], in_sems.at[y]
                    ).start()
    for y in range(LINES):
        pltpu.make_async_copy(held.at[y], held.at[y], in_sems.at[y]).wait()
        pltpu.make_async_copy(held.at[y], out_ref.at[y], out_sem).start()
    pltpu.make_async_copy(held, held, out_sem).wait()


def pick_call(kernel, scalars, operands, count, rows, name):
    shape = (LINES, count, rows, BLOCK)
    size = LINES * count * rows * BLOCK * 2
    return pl.pallas_call(
        kernel,
        grid_spec=pltpu.PrefetchScalarGridSpec(
            num_scalar_prefetch=len(scalars),
            grid=(1,),
            in_specs=[pl.BlockSpec(memory_space=pltpu.HBM)] * len(operands),
            out_specs=pl.BlockSpec(memory_space=pltpu.HBM),
            scratch_shapes=[
                pltpu.VMEM(shape, jnp.bfloat16),
                pltpu.SemaphoreType.DMA((LINES,)),
                pltpu.SemaphoreType.DMA,
            ],
        ),
        out_shape=jax.ShapeDtypeStruct(shape, jnp.bfloat16),
        compiler_params=pltpu.CompilerParams(vmem_limit_bytes=PICK_VMEM),
        cost_estimate=pl.CostEstimate(
            flops=PICK_WEIGHT, bytes_accessed=2 * size, transcendentals=0
        ),
        name=name,
    )(*scalars, *operands)


def pick_part(ids, here, part, pieces, rows):
    flat = [array for ps in pieces for array, _ in ps]

    def kernel(ids_ref, here_ref, *refs):
        sources, (out_ref, held, in_sems, out_sem) = refs[:-4], refs[-4:]
        senders, at = [], 0
        for offset, ps in zip(part, pieces):
            z = (here_ref[0] + (offset + STEPS)) & (STEPS - 1)
            senders.append((z, [(sources[at + n], f) for n, (_, f) in enumerate(ps)]))
            at += len(ps)
        copy_blocks(ids_ref, senders, out_ref, held, in_sems, out_sem)

    return pick_call(kernel, (ids, here), flat, len(part) * CAP, rows, "pick_part")


def mix_early(codes, arrays, weights):
    per_device, taps = weights.shape[:2]
    rows = arrays[0].shape[1]
    total = sum(array.shape[0] for array in arrays)

    def kernel(codes_ref, *refs):
        blocks_refs = refs[: len(arrays)]
        weight_ref, out_ref, held, sem = refs[len(arrays) :]
        j = pl.program_id(0)
        here = held.at[pl.ds(0, total)]

        @pl.when(j == 0)
        def _():
            at = 0
            for ref in blocks_refs:
                pltpu.make_async_copy(ref, held.at[pl.ds(at, ref.shape[0])], sem).start()
                at += ref.shape[0]
            held[total] = jnp.zeros((rows, BLOCK), jnp.bfloat16)
            pltpu.make_async_copy(here, here, sem).wait()

        blocks = [
            held[jnp.minimum(codes_ref[j * taps + k], total)] for k in range(taps)
        ]
        out_ref[...] = jnp.dot(
            jnp.concatenate(blocks, axis=1),
            weight_ref[0].reshape(taps * BLOCK, BLOCK),
            preferred_element_type=jnp.float32,
        )

    return pl.pallas_call(
        kernel,
        grid_spec=pltpu.PrefetchScalarGridSpec(
            num_scalar_prefetch=1,
            grid=(per_device,),
            in_specs=[pl.BlockSpec(memory_space=pl.ANY)] * len(arrays)
            + [pl.BlockSpec((1, taps, BLOCK, BLOCK), lambda j, s: (j, 0, 0, 0))],
            out_specs=pl.BlockSpec((rows, BLOCK), lambda j, s: (0, j)),
            scratch_shapes=[
                pltpu.VMEM((total + 1, rows, BLOCK), jnp.bfloat16),
                pltpu.SemaphoreType.DMA,
            ],
        ),
        out_shape=jax.ShapeDtypeStruct((rows, per_device * BLOCK), jnp.float32),
        compiler_params=pltpu.CompilerParams(vmem_limit_bytes=MIX_VMEM),
        cost_estimate=pl.CostEstimate(
            flops=MIX_WEIGHT,
            bytes_accessed=(total * rows + per_device * taps * BLOCK) * BLOCK * 2,
            transcendentals=0,
        ),
        name="mix_early",
    )(codes, *arrays, weights)


def late_first(codes, base, per_device):
    places = codes.reshape(per_device, -1) - base
    taps = places.shape[1]
    late = places >= 0
    tap = jnp.arange(taps, dtype=jnp.int32)
    before = (tap[None, :, None] > tap[None, None, :]) & late[:, None, :]
    rank = jnp.sum(before.astype(jnp.int32), axis=2)
    chosen = late[:, None, :] & (rank[:, None, :] == tap[None, :, None])
    place = jnp.sum(jnp.where(chosen, places[:, None, :], 0), axis=2)
    which = jnp.sum(jnp.where(chosen, tap[None, None, :], 0), axis=2)
    count = jnp.sum(late.astype(jnp.int32), axis=1)
    return place.reshape(-1), which.reshape(-1), count


def mix_late(late, early, array, weights, bias, first, count):
    taps = weights.shape[1]
    size, rows = array.shape[:2]
    step = 4

    def kernel(
        place_ref, which_ref, count_ref, early_ref, blocks_ref, weight_ref, bias_ref, out_ref, total
    ):
        j = pl.program_id(0) + first
        total[...] = early_ref[...] + bias_ref[0]
        here = count_ref[j]
        for k in range(0, taps, step):

            @pl.when(k < here)
            def _(k=k):
                inputs, stack = [], []
                for i in range(k, k + step):
                    kept = jnp.where(i < here, 1.0, 0.0).astype(jnp.bfloat16)
                    inputs.append(blocks_ref[place_ref[j * taps + i]] * kept)
                    stack.append(weight_ref[0, which_ref[j * taps + i]])
                total[...] += jnp.dot(
                    jnp.concatenate(inputs, axis=1),
                    jnp.concatenate(stack, axis=0),
                    preferred_element_type=jnp.float32,
                )

        out_ref[...] = jnp.clip(total[...], 0.0, CLAMP_TOP).astype(jnp.bfloat16)

    return pl.pallas_call(
        kernel,
        grid_spec=pltpu.PrefetchScalarGridSpec(
            num_scalar_prefetch=3,
            grid=(count,),
            in_specs=[
                pl.BlockSpec((rows, BLOCK), lambda j, *s: (0, j + first)),
                pl.BlockSpec(memory_space=pltpu.VMEM),
                pl.BlockSpec(
                    (1, taps, BLOCK, BLOCK), lambda j, *s: (j + first, 0, 0, 0)
                ),
                pl.BlockSpec((1, 1, BLOCK), lambda j, *s: (j + first, 0, 0)),
            ],
            out_specs=pl.BlockSpec((rows, BLOCK), lambda j, *s: (0, j)),
            scratch_shapes=[pltpu.VMEM((rows, BLOCK), jnp.float32)],
        ),
        out_shape=jax.ShapeDtypeStruct((rows, count * BLOCK), jnp.bfloat16),
        compiler_params=pltpu.CompilerParams(vmem_limit_bytes=LATE_VMEM),
        cost_estimate=pl.CostEstimate(
            flops=2 * rows * count * taps * BLOCK * BLOCK,
            bytes_accessed=(size * rows + count * taps * BLOCK) * BLOCK * 2,
            transcendentals=0,
        ),
        name="mix_late",
    )(*late, early, array, weights, bias.reshape(-1, 1, BLOCK))


def shifted(value, axis, by):
    count = lax.axis_size(axis)
    return lax.ppermute(value, axis, [(i, (i + by) % count) for i in range(count)])


def over_lines(outgoing):
    incoming = lax.all_to_all(outgoing, "y", 0, 0, tiled=True)
    return incoming.reshape((-1,) + incoming.shape[2:])


def part_codes(slots, here):
    line, z, c = slots >> 5, (slots >> 1) & (STEPS - 1), slots & 1
    offset = (z - here) & (STEPS - 1)
    codes = jnp.zeros_like(slots)
    base = 0
    for part in PARTS:
        for i, o in enumerate(part):
            code = base + line * (len(part) * CAP) + i * CAP + c
            codes = jnp.where(offset == o % STEPS, code, codes)
        base += LINES * len(part) * CAP
    return codes


def body(layer_input, weight_blocks, neuron_bias, block_slots, send_lists):
    samples, weights, bias = layer_input[0], weight_blocks[0], neuron_bias[0]
    slots = block_slots.reshape(-1)
    here = lax.axis_index(Z).astype(jnp.int32)
    lists = send_lists.reshape(LINES, GROUP, GROUP, CAP).transpose(2, 1, 0, 3)

    held = {0: [(samples, 0)]}
    up = down = samples
    picked, arrived = [], []

    def pick_next():
        part = PARTS[len(picked)]
        pieces = [held[o] for o in part]
        picked.append(pick_part(ids, here.reshape(1), part, pieces, samples.shape[0]))

    def send_next():
        arrived.append(over_lines(picked[len(arrived)]))

    near = lax.all_to_all(lists, "near", 0, 0, tiled=True)
    last = STEPS // 2
    half = samples.shape[0] // 32 * 16
    ready = []
    for step in range(1, last + 1):
        if step == 2:
            near, up, down = lax.optimization_barrier((near, up, down))
            far = near.transpose(1, 0, 2, 3)
            ids = lax.all_to_all(far, "far", 0, 0, tiled=True).reshape(-1)
        for index, done in enumerate(ready):
            if step == done + 2:
                pick_next()
                picked[index], up, down = lax.optimization_barrier(
                    (picked[index], up, down)
                )
                if index in AFTER:
                    picked[index], arrived[-1] = lax.optimization_barrier(
                        (picked[index], arrived[-1])
                    )
                send_next()
            if step == HAVE[index]:
                arrived[index], up, down = lax.optimization_barrier(
                    (arrived[index], up, down)
                )
        if step < last:
            up, down = shifted(up, Z, 1), shifted(down, Z, -1)
            held[-step], held[step] = [(up, 0)], [(down, 0)]
        else:
            up, down = shifted(up[:half], Z, 1), shifted(down[half:], Z, -1)
            held[step] = [(up, 0), (down, half)]
        if all(o in held for o in PARTS[len(ready)]):
            ready.append(step)
    pick_next()
    send_next()

    codes = part_codes(slots, here)
    early = mix_early(codes, arrived[:-1], weights)
    base = sum(array.shape[0] for array in arrived[:-1])
    late = late_first(codes, base, weights.shape[0])
    cut = weights.shape[0] * 5 // 8
    outs = [
        mix_late(late, early, arrived[-1], weights, bias, first, last - first)
        for first, last in ((0, cut), (cut, weights.shape[0]))
    ]
    outs = [shifted(out, "segment", 1) for out in outs]
    return jnp.concatenate(outs, axis=1)[None]


def solution(mesh):
    segments, row = mesh.devices.shape
    split = Mesh(
        mesh.devices.reshape(segments, row // STEPS, GROUP, GROUP), ("segment", "y", *Z)
    )
    row = ("y", *Z)
    placed = (
        P("segment", None, row),
        P("segment", row, None, None, None),
        P("segment", row),
        P("segment", row, None),
        P("segment", row, None, None),
    )
    return jax.shard_map(
        body,
        mesh=split,
        in_specs=placed,
        out_specs=P("segment", None, row),
        check_vma=False,
    )
```

```python
import jax
import jax.numpy as jnp
from jax import lax
from jax.experimental import pallas as pl
from jax.experimental.pallas import tpu as pltpu
from jax.sharding import Mesh, PartitionSpec as P

CLAMP_TOP = 3.0
LINES = 4
STEPS = 16
GROUP = 4
Z = ("far", "near")
CAP = 2
BLOCK = 128
PICK_VMEM = 24 * 2**20
MIX_VMEM = 50 * 2**20
LATE_VMEM = 50 * 2**20
MIX_WEIGHT = 10**10
PICK_WEIGHT = 12 * 10**9
AFTER = (2,)
HAVE = (5, 8, 9, 9)
PARTS = (
    (0, -1, 1),
    (-2, 2, -3, 3),
    (-4, 4, -5, 5),
    (-6, 6, -7, 7, 8),
)


def copy_blocks(ids_ref, senders, out_ref, held, in_sems, out_sem):
    for y in range(LINES):
        for i, (z, pieces) in enumerate(senders):
            for c in range(CAP):
                block = ids_ref[(z * LINES + y) * CAP + c] & 7
                columns = pl.ds(pl.multiple_of(block * BLOCK, BLOCK), BLOCK)
                for ref, first in pieces:
                    rows = pl.ds(first, ref.shape[0])
                    pltpu.make_async_copy(
                        ref.at[:, columns], held.at[y, i * CAP + c, rows], in_sems.at[y]
                    ).start()
    for y in range(LINES):
        pltpu.make_async_copy(held.at[y], held.at[y], in_sems.at[y]).wait()
        pltpu.make_async_copy(held.at[y], out_ref.at[y], out_sem).start()
    pltpu.make_async_copy(held, held, out_sem).wait()


def pick_call(kernel, scalars, operands, count, rows, name, vmem):
    shape = (LINES, count, rows, BLOCK)
    size = LINES * count * rows * BLOCK * 2
    return pl.pallas_call(
        kernel,
        grid_spec=pltpu.PrefetchScalarGridSpec(
            num_scalar_prefetch=len(scalars),
            grid=(1,),
            in_specs=[pl.BlockSpec(memory_space=pltpu.HBM)] * len(operands),
            out_specs=pl.BlockSpec(memory_space=pltpu.HBM),
            scratch_shapes=[
                pltpu.VMEM(shape, jnp.bfloat16),
                pltpu.SemaphoreType.DMA((LINES,)),
                pltpu.SemaphoreType.DMA,
            ],
        ),
        out_shape=jax.ShapeDtypeStruct(shape, jnp.bfloat16),
        compiler_params=pltpu.CompilerParams(vmem_limit_bytes=vmem),
        cost_estimate=pl.CostEstimate(
            flops=PICK_WEIGHT, bytes_accessed=2 * size, transcendentals=0
        ),
        name=name,
    )(*scalars, *operands)


def pick_part(ids, here, part, pieces, rows):
    flat = [array for ps in pieces for array, _ in ps]

    def kernel(ids_ref, here_ref, *refs):
        sources, (out_ref, held, in_sems, out_sem) = refs[:-4], refs[-4:]
        senders, at = [], 0
        for offset, ps in zip(part, pieces):
            z = (here_ref[0] + (offset + STEPS)) & (STEPS - 1)
            senders.append((z, [(sources[at + n], f) for n, (_, f) in enumerate(ps)]))
            at += len(ps)
        copy_blocks(ids_ref, senders, out_ref, held, in_sems, out_sem)

    vmem = MIX_VMEM if part == PARTS[-1] else PICK_VMEM
    return pick_call(kernel, (ids, here), flat, len(part) * CAP, rows, "pick_part", vmem)


def mix_early(codes, arrays, weights):
    per_device, taps = weights.shape[:2]
    rows = arrays[0].shape[1]
    total = sum(array.shape[0] for array in arrays)

    def kernel(codes_ref, *refs):
        blocks_refs = refs[: len(arrays)]
        weight_ref, out_ref, held, sem = refs[len(arrays) :]
        j = pl.program_id(0)
        here = held.at[pl.ds(0, total)]

        @pl.when(j == 0)
        def _():
            at = 0
            for ref in blocks_refs:
                pltpu.make_async_copy(ref, held.at[pl.ds(at, ref.shape[0])], sem).start()
                at += ref.shape[0]
            held[total] = jnp.zeros((rows, BLOCK), jnp.bfloat16)
            pltpu.make_async_copy(here, here, sem).wait()

        blocks = [
            held[jnp.minimum(codes_ref[j * taps + k], total)] for k in range(taps)
        ]
        out_ref[...] = jnp.dot(
            jnp.concatenate(blocks, axis=1),
            weight_ref[0].reshape(taps * BLOCK, BLOCK),
            preferred_element_type=jnp.float32,
        )

    return pl.pallas_call(
        kernel,
        grid_spec=pltpu.PrefetchScalarGridSpec(
            num_scalar_prefetch=1,
            grid=(per_device,),
            in_specs=[pl.BlockSpec(memory_space=pl.ANY)] * len(arrays)
            + [pl.BlockSpec((1, taps, BLOCK, BLOCK), lambda j, s: (j, 0, 0, 0))],
            out_specs=pl.BlockSpec((rows, BLOCK), lambda j, s: (0, j)),
            scratch_shapes=[
                pltpu.VMEM((total + 1, rows, BLOCK), jnp.bfloat16),
                pltpu.SemaphoreType.DMA,
            ],
        ),
        out_shape=jax.ShapeDtypeStruct((rows, per_device * BLOCK), jnp.float32),
        compiler_params=pltpu.CompilerParams(vmem_limit_bytes=MIX_VMEM),
        cost_estimate=pl.CostEstimate(
            flops=MIX_WEIGHT,
            bytes_accessed=(total * rows + per_device * taps * BLOCK) * BLOCK * 2,
            transcendentals=0,
        ),
        name="mix_early",
    )(codes, *arrays, weights)


def late_first(codes, base, per_device):
    places = codes.reshape(per_device, -1) - base
    taps = places.shape[1]
    late = places >= 0
    tap = jnp.arange(taps, dtype=jnp.int32)
    before = (tap[None, :, None] > tap[None, None, :]) & late[:, None, :]
    rank = jnp.sum(before.astype(jnp.int32), axis=2)
    chosen = late[:, None, :] & (rank[:, None, :] == tap[None, :, None])
    place = jnp.sum(jnp.where(chosen, places[:, None, :], 0), axis=2)
    which = jnp.sum(jnp.where(chosen, tap[None, None, :], 0), axis=2)
    count = jnp.sum(late.astype(jnp.int32), axis=1)
    return place.reshape(-1), which.reshape(-1), count


def mix_late(late, early, array, weights, bias, first, count):
    taps = weights.shape[1]
    size, rows = array.shape[:2]
    step = 4

    def kernel(
        place_ref, which_ref, count_ref, early_ref, blocks_ref, weight_ref, bias_ref, out_ref, total
    ):
        j = pl.program_id(0) + first
        total[...] = early_ref[...] + bias_ref[0]
        here = count_ref[j]
        for k in range(0, taps, step):

            @pl.when(k < here)
            def _(k=k):
                inputs, stack = [], []
                for i in range(k, k + step):
                    kept = jnp.where(i < here, 1.0, 0.0).astype(jnp.bfloat16)
                    inputs.append(blocks_ref[place_ref[j * taps + i]] * kept)
                    stack.append(weight_ref[0, which_ref[j * taps + i]])
                total[...] += jnp.dot(
                    jnp.concatenate(inputs, axis=1),
                    jnp.concatenate(stack, axis=0),
                    preferred_element_type=jnp.float32,
                )

        out_ref[...] = jnp.clip(total[...], 0.0, CLAMP_TOP).astype(jnp.bfloat16)

    return pl.pallas_call(
        kernel,
        grid_spec=pltpu.PrefetchScalarGridSpec(
            num_scalar_prefetch=3,
            grid=(count,),
            in_specs=[
                pl.BlockSpec((rows, BLOCK), lambda j, *s: (0, j + first)),
                pl.BlockSpec(memory_space=pltpu.VMEM),
                pl.BlockSpec(
                    (1, taps, BLOCK, BLOCK), lambda j, *s: (j + first, 0, 0, 0)
                ),
                pl.BlockSpec((1, 1, BLOCK), lambda j, *s: (j + first, 0, 0)),
            ],
            out_specs=pl.BlockSpec((rows, BLOCK), lambda j, *s: (0, j)),
            scratch_shapes=[pltpu.VMEM((rows, BLOCK), jnp.float32)],
        ),
        out_shape=jax.ShapeDtypeStruct((rows, count * BLOCK), jnp.bfloat16),
        compiler_params=pltpu.CompilerParams(vmem_limit_bytes=LATE_VMEM),
        cost_estimate=pl.CostEstimate(
            flops=2 * rows * count * taps * BLOCK * BLOCK,
            bytes_accessed=(size * rows + count * taps * BLOCK) * BLOCK * 2,
            transcendentals=0,
        ),
        name="mix_late",
    )(*late, early, array, weights, bias.reshape(-1, 1, BLOCK))


def shifted(value, axis, by):
    count = lax.axis_size(axis)
    return lax.ppermute(value, axis, [(i, (i + by) % count) for i in range(count)])


def over_lines(outgoing):
    incoming = lax.all_to_all(outgoing, "y", 0, 0, tiled=True)
    return incoming.reshape((-1,) + incoming.shape[2:])


def part_codes(slots, here):
    line, z, c = slots >> 5, (slots >> 1) & (STEPS - 1), slots & 1
    offset = (z - here) & (STEPS - 1)
    codes = jnp.zeros_like(slots)
    base = 0
    for part in PARTS:
        for i, o in enumerate(part):
            code = base + line * (len(part) * CAP) + i * CAP + c
            codes = jnp.where(offset == o % STEPS, code, codes)
        base += LINES * len(part) * CAP
    return codes


def body(layer_input, weight_blocks, neuron_bias, block_slots, send_lists):
    samples, weights, bias = layer_input[0], weight_blocks[0], neuron_bias[0]
    slots = block_slots.reshape(-1)
    here = lax.axis_index(Z).astype(jnp.int32)
    lists = send_lists.reshape(LINES, GROUP, GROUP, CAP).transpose(2, 1, 0, 3)

    held = {0: [(samples, 0)]}
    up = down = samples
    picked, arrived = [], []

    def pick_next():
        part = PARTS[len(picked)]
        pieces = [held[o] for o in part]
        picked.append(pick_part(ids, here.reshape(1), part, pieces, samples.shape[0]))

    def send_next():
        arrived.append(over_lines(picked[len(arrived)]))

    near = lax.all_to_all(lists, "near", 0, 0, tiled=True)
    last = STEPS // 2
    half = samples.shape[0] // 32 * 16
    ready = []
    for step in range(1, last + 1):
        if step == 2:
            near, up, down = lax.optimization_barrier((near, up, down))
            far = near.transpose(1, 0, 2, 3)
            ids = lax.all_to_all(far, "far", 0, 0, tiled=True).reshape(-1)
        for index, done in enumerate(ready):
            if step == done + 2:
                pick_next()
                picked[index], up, down = lax.optimization_barrier(
                    (picked[index], up, down)
                )
                if index in AFTER:
                    picked[index], arrived[-1] = lax.optimization_barrier(
                        (picked[index], arrived[-1])
                    )
                send_next()
            if step == HAVE[index]:
                arrived[index], up, down = lax.optimization_barrier(
                    (arrived[index], up, down)
                )
        if step < last:
            up, down = shifted(up, Z, 1), shifted(down, Z, -1)
            held[-step], held[step] = [(up, 0)], [(down, 0)]
        else:
            up, down = shifted(up[:half], Z, 1), shifted(down[half:], Z, -1)
            held[step] = [(up, 0), (down, half)]
        if all(o in held for o in PARTS[len(ready)]):
            ready.append(step)
    pick_next()
    send_next()

    codes = part_codes(slots, here)
    early = mix_early(codes, arrived[:-1], weights)
    base = sum(array.shape[0] for array in arrived[:-1])
    late = late_first(codes, base, weights.shape[0])
    cut = weights.shape[0] * 5 // 8
    outs = [
        mix_late(late, early, arrived[-1], weights, bias, first, last - first)
        for first, last in ((0, cut), (cut, weights.shape[0]))
    ]
    outs = [shifted(out, "segment", 1) for out in outs]
    return jnp.concatenate(outs, axis=1)[None]


def solution(mesh):
    segments, row = mesh.devices.shape
    split = Mesh(
        mesh.devices.reshape(segments, row // STEPS, GROUP, GROUP), ("segment", "y", *Z)
    )
    row = ("y", *Z)
    placed = (
        P("segment", None, row),
        P("segment", row, None, None, None),
        P("segment", row),
        P("segment", row, None),
        P("segment", row, None, None),
    )
    return jax.shard_map(
        body,
        mesh=split,
        in_specs=placed,
        out_specs=P("segment", None, row),
        check_vma=False,
    )
```

```python
import jax
import jax.numpy as jnp
from jax import lax
from jax.experimental import pallas as pl
from jax.experimental.pallas import tpu as pltpu
from jax.sharding import Mesh, PartitionSpec as P

CLAMP_TOP = 3.0
LINES = 4
STEPS = 16
GROUP = 4
Z = ("far", "near")
CAP = 2
BLOCK = 128
PICK_VMEM = 24 * 2**20
MIX_VMEM = 50 * 2**20
LATE_VMEM = 50 * 2**20
MIX_WEIGHT = 10**10
PICK_WEIGHT = 12 * 10**9
AFTER = (2, 3)
HAVE = (5, 8, 9, 9, 9)
PARTS = (
    (0, -1, 1),
    (-2, 2, -3, 3),
    (-4, 4, -5, 5),
    (-6, 6),
    (-7, 7, 8),
)


def copy_blocks(ids_ref, senders, out_ref, held, in_sems, out_sem):
    for y in range(LINES):
        for i, (z, pieces) in enumerate(senders):
            for c in range(CAP):
                block = ids_ref[(z * LINES + y) * CAP + c] & 7
                columns = pl.ds(pl.multiple_of(block * BLOCK, BLOCK), BLOCK)
                for ref, first in pieces:
                    rows = pl.ds(first, ref.shape[0])
                    pltpu.make_async_copy(
                        ref.at[:, columns], held.at[y, i * CAP + c, rows], in_sems.at[y]
                    ).start()
    for y in range(LINES):
        pltpu.make_async_copy(held.at[y], held.at[y], in_sems.at[y]).wait()
        pltpu.make_async_copy(held.at[y], out_ref.at[y], out_sem).start()
    pltpu.make_async_copy(held, held, out_sem).wait()


def pick_call(kernel, scalars, operands, count, rows, name):
    shape = (LINES, count, rows, BLOCK)
    size = LINES * count * rows * BLOCK * 2
    return pl.pallas_call(
        kernel,
        grid_spec=pltpu.PrefetchScalarGridSpec(
            num_scalar_prefetch=len(scalars),
            grid=(1,),
            in_specs=[pl.BlockSpec(memory_space=pltpu.HBM)] * len(operands),
            out_specs=pl.BlockSpec(memory_space=pltpu.HBM),
            scratch_shapes=[
                pltpu.VMEM(shape, jnp.bfloat16),
                pltpu.SemaphoreType.DMA((LINES,)),
                pltpu.SemaphoreType.DMA,
            ],
        ),
        out_shape=jax.ShapeDtypeStruct(shape, jnp.bfloat16),
        compiler_params=pltpu.CompilerParams(vmem_limit_bytes=PICK_VMEM),
        cost_estimate=pl.CostEstimate(
            flops=PICK_WEIGHT, bytes_accessed=2 * size, transcendentals=0
        ),
        name=name,
    )(*scalars, *operands)


def pick_part(ids, here, part, pieces, rows):
    flat = [array for ps in pieces for array, _ in ps]

    def kernel(ids_ref, here_ref, *refs):
        sources, (out_ref, held, in_sems, out_sem) = refs[:-4], refs[-4:]
        senders, at = [], 0
        for offset, ps in zip(part, pieces):
            z = (here_ref[0] + (offset + STEPS)) & (STEPS - 1)
            senders.append((z, [(sources[at + n], f) for n, (_, f) in enumerate(ps)]))
            at += len(ps)
        copy_blocks(ids_ref, senders, out_ref, held, in_sems, out_sem)

    return pick_call(kernel, (ids, here), flat, len(part) * CAP, rows, "pick_part")


def mix_early(codes, arrays, weights):
    per_device, taps = weights.shape[:2]
    rows = arrays[0].shape[1]
    total = sum(array.shape[0] for array in arrays)

    def kernel(codes_ref, *refs):
        blocks_refs = refs[: len(arrays)]
        weight_ref, out_ref, held, sem = refs[len(arrays) :]
        j = pl.program_id(0)
        here = held.at[pl.ds(0, total)]

        @pl.when(j == 0)
        def _():
            at = 0
            for ref in blocks_refs:
                pltpu.make_async_copy(ref, held.at[pl.ds(at, ref.shape[0])], sem).start()
                at += ref.shape[0]
            held[total] = jnp.zeros((rows, BLOCK), jnp.bfloat16)
            pltpu.make_async_copy(here, here, sem).wait()

        blocks = [
            held[jnp.minimum(codes_ref[j * taps + k], total)] for k in range(taps)
        ]
        out_ref[...] = jnp.dot(
            jnp.concatenate(blocks, axis=1),
            weight_ref[0].reshape(taps * BLOCK, BLOCK),
            preferred_element_type=jnp.float32,
        )

    return pl.pallas_call(
        kernel,
        grid_spec=pltpu.PrefetchScalarGridSpec(
            num_scalar_prefetch=1,
            grid=(per_device,),
            in_specs=[pl.BlockSpec(memory_space=pl.ANY)] * len(arrays)
            + [pl.BlockSpec((1, taps, BLOCK, BLOCK), lambda j, s: (j, 0, 0, 0))],
            out_specs=pl.BlockSpec((rows, BLOCK), lambda j, s: (0, j)),
            scratch_shapes=[
                pltpu.VMEM((total + 1, rows, BLOCK), jnp.bfloat16),
                pltpu.SemaphoreType.DMA,
            ],
        ),
        out_shape=jax.ShapeDtypeStruct((rows, per_device * BLOCK), jnp.float32),
        compiler_params=pltpu.CompilerParams(vmem_limit_bytes=MIX_VMEM),
        cost_estimate=pl.CostEstimate(
            flops=MIX_WEIGHT,
            bytes_accessed=(total * rows + per_device * taps * BLOCK) * BLOCK * 2,
            transcendentals=0,
        ),
        name="mix_early",
    )(codes, *arrays, weights)


def late_first(codes, base, per_device):
    places = codes.reshape(per_device, -1) - base
    taps = places.shape[1]
    late = places >= 0
    tap = jnp.arange(taps, dtype=jnp.int32)
    before = (tap[None, :, None] > tap[None, None, :]) & late[:, None, :]
    rank = jnp.sum(before.astype(jnp.int32), axis=2)
    chosen = late[:, None, :] & (rank[:, None, :] == tap[None, :, None])
    place = jnp.sum(jnp.where(chosen, places[:, None, :], 0), axis=2)
    which = jnp.sum(jnp.where(chosen, tap[None, None, :], 0), axis=2)
    count = jnp.sum(late.astype(jnp.int32), axis=1)
    return place.reshape(-1), which.reshape(-1), count


def mix_late(late, early, array, weights, bias, first, count):
    taps = weights.shape[1]
    size, rows = array.shape[:2]
    step = 4

    def kernel(
        place_ref, which_ref, count_ref, early_ref, blocks_ref, weight_ref, bias_ref, out_ref, total
    ):
        j = pl.program_id(0) + first
        total[...] = early_ref[...] + bias_ref[0]
        here = count_ref[j]
        for k in range(0, taps, step):

            @pl.when(k < here)
            def _(k=k):
                inputs, stack = [], []
                for i in range(k, k + step):
                    kept = jnp.where(i < here, 1.0, 0.0).astype(jnp.bfloat16)
                    inputs.append(blocks_ref[place_ref[j * taps + i]] * kept)
                    stack.append(weight_ref[0, which_ref[j * taps + i]])
                total[...] += jnp.dot(
                    jnp.concatenate(inputs, axis=1),
                    jnp.concatenate(stack, axis=0),
                    preferred_element_type=jnp.float32,
                )

        out_ref[...] = jnp.clip(total[...], 0.0, CLAMP_TOP).astype(jnp.bfloat16)

    return pl.pallas_call(
        kernel,
        grid_spec=pltpu.PrefetchScalarGridSpec(
            num_scalar_prefetch=3,
            grid=(count,),
            in_specs=[
                pl.BlockSpec((rows, BLOCK), lambda j, *s: (0, j + first)),
                pl.BlockSpec(memory_space=pltpu.VMEM),
                pl.BlockSpec(
                    (1, taps, BLOCK, BLOCK), lambda j, *s: (j + first, 0, 0, 0)
                ),
                pl.BlockSpec((1, 1, BLOCK), lambda j, *s: (j + first, 0, 0)),
            ],
            out_specs=pl.BlockSpec((rows, BLOCK), lambda j, *s: (0, j)),
            scratch_shapes=[pltpu.VMEM((rows, BLOCK), jnp.float32)],
        ),
        out_shape=jax.ShapeDtypeStruct((rows, count * BLOCK), jnp.bfloat16),
        compiler_params=pltpu.CompilerParams(vmem_limit_bytes=LATE_VMEM),
        cost_estimate=pl.CostEstimate(
            flops=2 * rows * count * taps * BLOCK * BLOCK,
            bytes_accessed=(size * rows + count * taps * BLOCK) * BLOCK * 2,
            transcendentals=0,
        ),
        name="mix_late",
    )(*late, early, array, weights, bias.reshape(-1, 1, BLOCK))


def shifted(value, axis, by):
    count = lax.axis_size(axis)
    return lax.ppermute(value, axis, [(i, (i + by) % count) for i in range(count)])


def over_lines(outgoing):
    incoming = lax.all_to_all(outgoing, "y", 0, 0, tiled=True)
    return incoming.reshape((-1,) + incoming.shape[2:])


def part_codes(slots, here):
    line, z, c = slots >> 5, (slots >> 1) & (STEPS - 1), slots & 1
    offset = (z - here) & (STEPS - 1)
    codes = jnp.zeros_like(slots)
    base = 0
    for part in PARTS:
        for i, o in enumerate(part):
            code = base + line * (len(part) * CAP) + i * CAP + c
            codes = jnp.where(offset == o % STEPS, code, codes)
        base += LINES * len(part) * CAP
    return codes


def body(layer_input, weight_blocks, neuron_bias, block_slots, send_lists):
    samples, weights, bias = layer_input[0], weight_blocks[0], neuron_bias[0]
    slots = block_slots.reshape(-1)
    here = lax.axis_index(Z).astype(jnp.int32)
    lists = send_lists.reshape(LINES, GROUP, GROUP, CAP).transpose(2, 1, 0, 3)

    held = {0: [(samples, 0)]}
    up = down = samples
    picked, arrived = [], []

    def pick_next():
        part = PARTS[len(picked)]
        pieces = [held[o] for o in part]
        picked.append(pick_part(ids, here.reshape(1), part, pieces, samples.shape[0]))

    def send_next():
        arrived.append(over_lines(picked[len(arrived)]))

    near = lax.all_to_all(lists, "near", 0, 0, tiled=True)
    last = STEPS // 2
    half = samples.shape[0] // 32 * 16
    ready = []
    for step in range(1, last + 1):
        if step == 2:
            near, up, down = lax.optimization_barrier((near, up, down))
            far = near.transpose(1, 0, 2, 3)
            ids = lax.all_to_all(far, "far", 0, 0, tiled=True).reshape(-1)
        for index, done in enumerate(ready):
            if step == done + 2:
                pick_next()
                picked[index], up, down = lax.optimization_barrier(
                    (picked[index], up, down)
                )
                if index in AFTER:
                    picked[index], arrived[-1] = lax.optimization_barrier(
                        (picked[index], arrived[-1])
                    )
                send_next()
            if step == HAVE[index]:
                arrived[index], up, down = lax.optimization_barrier(
                    (arrived[index], up, down)
                )
        if step < last:
            up, down = shifted(up, Z, 1), shifted(down, Z, -1)
            held[-step], held[step] = [(up, 0)], [(down, 0)]
        else:
            up, down = shifted(up[:half], Z, 1), shifted(down[half:], Z, -1)
            held[step] = [(up, 0), (down, half)]
        if all(o in held for o in PARTS[len(ready)]):
            ready.append(step)
    pick_next()
    picked[-1], arrived[-1] = lax.optimization_barrier((picked[-1], arrived[-1]))
    send_next()

    codes = part_codes(slots, here)
    early = mix_early(codes, arrived[:-1], weights)
    base = sum(array.shape[0] for array in arrived[:-1])
    late = late_first(codes, base, weights.shape[0])
    cut = weights.shape[0] * 5 // 8
    outs = [
        mix_late(late, early, arrived[-1], weights, bias, first, last - first)
        for first, last in ((0, cut), (cut, weights.shape[0]))
    ]
    outs = [shifted(out, "segment", 1) for out in outs]
    return jnp.concatenate(outs, axis=1)[None]


def solution(mesh):
    segments, row = mesh.devices.shape
    split = Mesh(
        mesh.devices.reshape(segments, row // STEPS, GROUP, GROUP), ("segment", "y", *Z)
    )
    row = ("y", *Z)
    placed = (
        P("segment", None, row),
        P("segment", row, None, None, None),
        P("segment", row),
        P("segment", row, None),
        P("segment", row, None, None),
    )
    return jax.shard_map(
        body,
        mesh=split,
        in_specs=placed,
        out_specs=P("segment", None, row),
        check_vma=False,
    )
```
